128 devices in a mesh: rep: 16 (over y_lo, z, core), tp: 8 (over y_hi, x).
Axes of the slice: x: 4, y: 4 (y_hi: 2, y_lo: 2; y = y_hi * 2 + y_lo), z: 4, core: 2. Of those that a mesh axis runs over, the one named last changes fastest.
Arguments:
- hidden: bfloat16 [2, 32, 8192], P(None, 'rep'), may hold values from -6 to 6
- queries: bfloat16 [2, 32, 8192], P(None, 'rep', 'tp'), may hold values from -160 to 160
- sectioned: bfloat16 [8192, 2048], P('rep', 'tp'), may hold values from -0.0625 to 0.0625
- owners: int32 [16], replicated, may hold values from 0 to 15, each once
- rotated_key_cache: bfloat16 [32, 8192, 1024], P('rep', None, 'tp'), may hold values from -6 to 6
- stored_value_cache: bfloat16 [32, 8192, 1024], P('rep', None, 'tp'), may hold values from -6 to 6
- lengths: int32 [32], P('rep'), may hold values from 2 to 8190, as said below
- out_weight: bfloat16 [8192, 4096], P('tp'), may hold values from -0.71875 to 0.71875
Outputs:
- installed: bfloat16 [8192, 2048], P(None, 'tp')
- appended: bfloat16 [2, 32, 2048], P(None, 'rep', 'tp')
- attention_out: bfloat16 [2, 32, 4096], P(None, 'rep')
The draws below stay inside these ranges and needn't reach their ends.
Inputs may be any that keep to these rules, and one draw needn't show every extreme that they name: `lengths`: session 0 has the most filled slots.
All inputs are finite; a program needn't handle non-finite values.
Results may differ from the reference program's by a relative error of at most 0.0062.
Values may be sent and summed in bfloat16 or wider, within the bound.
A program may use at most 128 MiB of HBM per device.

```python
import jax
import jax.numpy as jnp
from jax import lax

MODEL_DIM = 8192
QUERY_HEADS = 64
KEY_HEADS = 8
HEAD_DIM = 128
DW = 4096
CACHE_CAPACITY = 8192
DECODE_STEPS = 2
QUERY_GROUP = 8
SESSION_COUNT = 32
N_REP = 16


def cache_base(key):
    return jnp.clip(jax.random.normal(key, (SESSION_COUNT, CACHE_CAPACITY, KEY_HEADS * HEAD_DIM), jnp.float32), -5.0, 5.0)


def draw_rotated_key_cache(key, part):
    starting_keys = cache_base(key)
    return starting_keys.astype(jnp.bfloat16)


def draw_queries(key, part):
    key = jax.random.fold_in(key, 5)
    drawn = jnp.clip(2.0 * jax.random.normal(key, (DECODE_STEPS, SESSION_COUNT, QUERY_HEADS * HEAD_DIM), jnp.float32), -12.0, 12.0)
    return drawn.astype(jnp.bfloat16)


def draw_lengths(key, part):
    key = jax.random.fold_in(key, 7)
    drawn = jax.random.randint(key, (SESSION_COUNT,), 2, CACHE_CAPACITY - DECODE_STEPS + 1, jnp.int32)
    return drawn.at[0].set(CACHE_CAPACITY - DECODE_STEPS)


def shard_levels(own_key, extent, pieces, smallest, high):
    loudness, own = 1.0, jax.random.fold_in(own_key, 6)
    for dim, blocks in pieces:
        heights = jnp.exp(jax.random.uniform(jax.random.fold_in(own, dim), (blocks,), jnp.float32, smallest / len(pieces), high / len(pieces)))
        loudness = loudness * jnp.repeat(heights, extent[dim] // blocks).reshape([-1 if axis == dim else 1 for axis in range(len(extent))])
    return loudness


def gaussian(rng, shape, scale, reach, shards=(), held_as=jnp.bfloat16):
    loudness = shard_levels(rng, shape, shards, -0.22, 0.18) if shards else 1.0
    array = jax.random.normal(rng, shape, jnp.float32) * scale * loudness
    return jnp.minimum(jnp.maximum(array, -reach), reach).astype(held_as)


def setup_inputs(seed: int = 0) -> dict:
    keys = jax.random.split(jax.random.key(seed), 9)
    hidden = gaussian(keys[0], (DECODE_STEPS, SESSION_COUNT, MODEL_DIM), 1.0, 6.0, ((1, 16),))
    queries = draw_queries(jax.random.fold_in(keys[8], 71), 0)
    sectioned = gaussian(keys[2], (MODEL_DIM, KEY_HEADS * 2 * HEAD_DIM), MODEL_DIM ** -0.5, 0.0625, ((0, 16), (1, 8)))
    owners = jax.random.permutation(keys[3], N_REP).astype(jnp.int32)
    rotated_key_cache = draw_rotated_key_cache(jax.random.fold_in(keys[8], 71), 0)
    stored_value_cache = gaussian(keys[5], (SESSION_COUNT, CACHE_CAPACITY, KEY_HEADS * HEAD_DIM), 1.0, 6.0, ((0, 16), (2, 8)))
    lengths = draw_lengths(jax.random.fold_in(keys[8], 71), 0)
    out_weight = gaussian(keys[7], (QUERY_HEADS * HEAD_DIM, DW), 0.12, 0.71875, ((0, 8),))
    return {"hidden": hidden, "queries": queries, "sectioned": sectioned, "owners": owners, "rotated_key_cache": rotated_key_cache, "stored_value_cache": stored_value_cache, "lengths": lengths, "out_weight": out_weight}


rope_base = 500000.0


def rotate(vectors, positions):
    halfway = vectors.shape[-1] // 2
    frequency = jnp.exp(-jnp.log(rope_base) * jnp.arange(halfway, dtype=jnp.float32) / halfway)
    angles = positions.astype(jnp.float32)[..., None] * frequency
    first_part = vectors[..., :halfway]
    second_part = vectors[..., halfway:]
    return jnp.concatenate([first_part * jnp.cos(angles) - second_part * jnp.sin(angles), second_part * jnp.cos(angles) + first_part * jnp.sin(angles)], axis=-1)


def reference(hidden, queries, sectioned, owners, rotated_key_cache, stored_value_cache, lengths, out_weight):
    block_list = sectioned.reshape(N_REP, MODEL_DIM // N_REP, KEY_HEADS * 2 * HEAD_DIM)
    installed = jnp.take(block_list, owners, axis=0).reshape(MODEL_DIM, KEY_HEADS * 2 * HEAD_DIM)
    projected_rows = jnp.dot(hidden.reshape(DECODE_STEPS * SESSION_COUNT, MODEL_DIM), installed, preferred_element_type=jnp.float32)
    projected_rows = projected_rows.reshape(DECODE_STEPS, SESSION_COUNT, KEY_HEADS, 2, HEAD_DIM)
    positions = lengths[None, :] + jnp.arange(DECODE_STEPS, dtype=jnp.int32)[:, None]
    incoming_keys = rotate(projected_rows[:, :, :, 0], positions[:, :, None]).astype(jnp.bfloat16)
    incoming_values = projected_rows[:, :, :, 1].astype(jnp.bfloat16)
    appended = jnp.stack([incoming_keys, incoming_values], axis=3).reshape(DECODE_STEPS, SESSION_COUNT, KEY_HEADS * 2 * HEAD_DIM)
    score_scale = HEAD_DIM ** -0.5
    causal_mask = jnp.arange(DECODE_STEPS)[None, :] <= jnp.arange(DECODE_STEPS)[:, None]

    def attend(session_index):
        query_head_rows = queries[:, session_index].astype(jnp.float32).reshape(DECODE_STEPS, KEY_HEADS, QUERY_GROUP, HEAD_DIM)
        stored_keys = rotated_key_cache[session_index].astype(jnp.float32).reshape(CACHE_CAPACITY, KEY_HEADS, HEAD_DIM)
        stored_values = stored_value_cache[session_index].astype(jnp.float32).reshape(CACHE_CAPACITY, KEY_HEADS, HEAD_DIM)
        fresh_keys = incoming_keys[:, session_index].astype(jnp.float32)
        fresh_values = incoming_values[:, session_index].astype(jnp.float32)
        scores_cache = jnp.einsum('tgqd,cgd->tgqc', query_head_rows, stored_keys) * score_scale
        valid_slots = jnp.arange(CACHE_CAPACITY, dtype=jnp.int32) < lengths[session_index]
        scores_cache = jnp.where(valid_slots[None, None, None, :], scores_cache, -jnp.inf)
        scores_new = jnp.einsum('tgqd,ugd->tgqu', query_head_rows, fresh_keys) * score_scale
        scores_new = jnp.where(causal_mask[:, None, None, :], scores_new, -jnp.inf)
        largest = jnp.maximum(jnp.max(scores_cache, axis=-1), jnp.max(scores_new, axis=-1))
        exp_cache = jnp.exp(scores_cache - largest[..., None])
        exp_new = jnp.exp(scores_new - largest[..., None])
        totals = jnp.sum(exp_cache, axis=-1) + jnp.sum(exp_new, axis=-1)
        weights_cache = (exp_cache / totals[..., None]).astype(jnp.bfloat16).astype(jnp.float32)
        weights_new = (exp_new / totals[..., None]).astype(jnp.bfloat16).astype(jnp.float32)
        attended = jnp.einsum('tgqc,cgd->tgqd', weights_cache, stored_values) + jnp.einsum('tgqu,ugd->tgqd', weights_new, fresh_values)
        return attended.astype(jnp.bfloat16).reshape(DECODE_STEPS, QUERY_HEADS * HEAD_DIM)

    heads_out = lax.map(attend, jnp.arange(SESSION_COUNT, dtype=jnp.int32))
    heads_out = jnp.transpose(heads_out, (1, 0, 2)).reshape(DECODE_STEPS * SESSION_COUNT, QUERY_HEADS * HEAD_DIM)
    attention_out = jnp.dot(heads_out, out_weight, preferred_element_type=jnp.float32)
    attention_out = attention_out.astype(jnp.bfloat16).reshape(DECODE_STEPS, SESSION_COUNT, DW)
    return installed, appended, attention_out
```

```python
import functools
import math

import jax
import jax.numpy as jnp
from jax import lax
from jax.experimental import pallas as pl
from jax.experimental.pallas import tpu as pltpu
from jax.sharding import PartitionSpec as P

HEAD_DIM = 128
ROPE_BASE = 500000.0
SCALE = HEAD_DIM**-0.5
MESH = pl.DeviceIdType.MESH
F32 = jnp.float32
BF16 = jnp.bfloat16

REPS = 16
TPS = 8
ROWS = 512
COLS = 256
STEPS = 2
SESSIONS = 2
TOKENS = STEPS * SESSIONS
GROUP = 8
QROWS = STEPS * GROUP
SLOTS = 8192
CHUNK = 2048
OUT_COLS = 512

A0 = (0, 144)
A1 = (144, 144)
A = (0, 288)
B0 = (288, 112)
B1 = (400, 112)
B = (288, 224)
WHOLE = (0, 512)


def frequencies(shape):
    lane = lax.broadcasted_iota(jnp.int32, shape, 1) % (HEAD_DIM // 2)
    result = jnp.ones(shape, F32)
    for bit in range(6):
        factor = math.exp(-math.log(ROPE_BASE) * (1 << bit) / (HEAD_DIM // 2))
        result = result * jnp.where((lane // (1 << bit)) % 2 == 1, factor, 1.0).astype(F32)
    return result


def main_kernel(
    hidden, queries, sectioned, owners, keys, values, lengths, weight,
    pooled, attended, appended,
    kbuf, vbuf, wbuf, hbuf, qbuf, own_s, len_s, hsplit, hsend, hrecv, hall, psend, precv,
    qrows, scores, heads, lhs, rsend, rrecv, gsend,
    load_sem, bulk_send, bulk_recv, sib_recv, small_send, small_recv,
):
    rep = lax.axis_index("rep")
    tp = lax.axis_index("tp")
    y, z, c = rep // 8, (rep // 2) % 4, rep % 2

    def chip(yy, zz, cc):
        return yy * 8 + lax.rem(zz + 4, 4) * 2 + cc

    zp = (chip(y, z + 1, c), tp)
    zm = (chip(y, z - 1, c), tp)
    yn = (chip(1 - y, z, c), tp)
    sib = (chip(y, z, 1 - c), tp)

    barrier = pltpu.get_barrier_semaphore()
    for k in range(1, REPS):
        pl.semaphore_signal(barrier, inc=1, device_id=(lax.rem(rep + k, REPS), tp), device_id_type=MESH)
    for k in range(1, TPS):
        pl.semaphore_signal(barrier, inc=1, device_id=(rep, lax.rem(tp + k, TPS)), device_id_type=MESH)

    loads = [
        pltpu.make_async_copy(owners, own_s, load_sem.at[0]),
        pltpu.make_async_copy(hidden, hbuf, load_sem.at[1]),
        pltpu.make_async_copy(sectioned, pooled.at[rep], load_sem.at[2]),
        pltpu.make_async_copy(lengths, len_s, load_sem.at[3]),
        pltpu.make_async_copy(queries, qbuf, load_sem.at[4]),
        pltpu.make_async_copy(keys.at[0], kbuf.at[0], load_sem.at[5]),
        pltpu.make_async_copy(keys.at[1], kbuf.at[1], load_sem.at[6]),
        pltpu.make_async_copy(values.at[0], vbuf.at[0], load_sem.at[7]),
        pltpu.make_async_copy(values.at[1], vbuf.at[1], load_sem.at[8]),
        pltpu.make_async_copy(weight, wbuf, load_sem.at[9]),
    ]
    for load in loads:
        load.start()

    loads[0].wait()
    loads[1].wait()
    for s in range(REPS):
        for t in range(STEPS):
            hsplit[s, pl.ds(t * SESSIONS, SESSIONS), :] = hbuf[t, :, pl.ds(s * ROWS, ROWS)].astype(F32)
    owner = [own_s[s] for s in range(REPS)]
    for r in range(REPS):
        place = jnp.int32(0)
        for s in range(1, REPS):
            place = jnp.where(owner[s] == r, s, place)
        hsend[r] = hsplit[place].astype(BF16)

    loads[4].wait()
    for s in range(SESSIONS):
        for t in range(STEPS):
            for q in range(GROUP):
                qrows[s, pl.ds(t * GROUP + q, 1), :] = qbuf[t, pl.ds(s, 1), pl.ds(q * HEAD_DIM, HEAD_DIM)].astype(F32)
    loads[2].wait()
    pl.semaphore_wait(barrier, REPS - 1 + TPS - 1)

    def small(src, dst, which, device):
        return pltpu.make_async_remote_copy(
            src_ref=src, dst_ref=dst, send_sem=small_send.at[which], recv_sem=small_recv.at[which],
            device_id=device, device_id_type=MESH)

    for k in range(1, REPS):
        peer = lax.rem(rep + k, REPS)
        small(hsend.at[peer], hrecv.at[rep], 0, (peer, tp)).start()
    hrecv[rep] = hsend[rep]

    def piece(block, part):
        return pooled.at[block, pl.ds(*part), :]

    def send(block, part, device, slot):
        ref = piece(block, part)
        pltpu.make_async_remote_copy(
            src_ref=ref, dst_ref=ref, send_sem=bulk_send, recv_sem=bulk_recv.at[slot],
            device_id=device, device_id_type=MESH).start()

    def to_sibling(block, part):
        ref = piece(block, part)
        pltpu.make_async_remote_copy(
            src_ref=ref, dst_ref=ref, send_sem=bulk_send, recv_sem=sib_recv,
            device_id=sib, device_id_type=MESH).start()

    def arrived(block, part, slot):
        ref = piece(block, part)
        pltpu.make_async_copy(ref, ref, bulk_recv.at[slot]).wait()

    here = {
        0: chip(y, z, c), 1: chip(y, z + 1, c), -1: chip(y, z - 1, c), 2: chip(y, z + 2, c)}
    there = {
        0: chip(1 - y, z, c), 1: chip(1 - y, z + 1, c), -1: chip(1 - y, z - 1, c), 2: chip(1 - y, z + 2, c)}

    send(here[0], B, zp, 1)
    send(here[0], B, zm, 2)
    send(here[0], A, yn, 3)
    send(here[0], A, zp, 4)
    send(here[0], A, zm, 5)
    send(here[0], B, yn, 14)
    to_sibling(here[0], WHOLE)

    def event(n):
        if n == 1:
            arrived(here[-1], B, 1)
            send(here[-1], B0, zp, 6)
            send(here[-1], B, yn, 15)
            to_sibling(here[-1], B)
        elif n == 2:
            arrived(here[1], B, 2)
            send(here[1], B1, zm, 7)
            send(here[1], B, yn, 16)
            to_sibling(here[1], B)
        elif n == 3:
            arrived(there[0], A, 3)
            send(there[0], A, zp, 8)
            send(there[0], A, zm, 9)
            to_sibling(there[0], A)
        elif n == 4:
            arrived(here[-1], A, 4)
            send(here[-1], A0, zp, 10)
            to_sibling(here[-1], A)
        elif n == 5:
            arrived(here[1], A, 5)
            send(here[1], A1, zm, 11)
            to_sibling(here[1], A)
        elif n == 6:
            arrived(here[2], B0, 6)
            send(here[2], B0, yn, 17)
            to_sibling(here[2], B0)
        elif n == 7:
            arrived(here[2], B1, 7)
            send(here[2], B1, yn, 18)
            to_sibling(here[2], B1)
        elif n == 8:
            arrived(there[-1], A, 8)
            send(there[-1], A0, zp, 12)
            to_sibling(there[-1], A)
        elif n == 9:
            arrived(there[1], A, 9)
            send(there[1], A1, zm, 13)
            to_sibling(there[1], A)
        else:
            block, part = {
                10: (here[2], A0), 11: (here[2], A1), 12: (there[2], A0), 13: (there[2], A1), 14: (there[0], B),
                15: (there[-1], B), 16: (there[1], B), 17: (there[2], B0), 18: (there[2], B1)}[n]
            arrived(block, part, n)
            to_sibling(block, part)

    loads[3].wait()
    length = [len_s[s] for s in range(SESSIONS)]

    def score(s):
        loads[5 + s].wait()
        q = qrows[s].astype(BF16)
        largest = jnp.full((QROWS, HEAD_DIM), -jnp.inf, F32)
        for i in range(SLOTS // CHUNK):
            part = lax.dot_general(
                q, kbuf[s, pl.ds(i * CHUNK, CHUNK), :], (((1,), (1,)), ((), ())), preferred_element_type=F32) * SCALE
            slot = lax.broadcasted_iota(jnp.int32, (QROWS, CHUNK), 1) + i * CHUNK
            part = jnp.where(slot < length[s], part, -jnp.inf)
            scores[s, :, pl.ds(i * CHUNK, CHUNK)] = part
            for j in range(CHUNK // HEAD_DIM):
                largest = jnp.maximum(largest, part[:, j * HEAD_DIM : (j + 1) * HEAD_DIM])
        return jnp.max(largest, axis=1, keepdims=True)

    def weigh(s, top):
        loads[7 + s].wait()
        total = jnp.zeros((QROWS, HEAD_DIM), F32)
        acc = jnp.zeros((QROWS, HEAD_DIM), F32)
        for i in range(SLOTS // CHUNK):
            p = jnp.exp(scores[s, :, pl.ds(i * CHUNK, CHUNK)] - top)
            for j in range(CHUNK // HEAD_DIM):
                total = total + p[:, j * HEAD_DIM : (j + 1) * HEAD_DIM]
            acc = acc + jnp.dot(p.astype(BF16), vbuf[s, pl.ds(i * CHUNK, CHUNK), :], preferred_element_type=F32)
        return jnp.sum(total, axis=1, keepdims=True), acc

    top = [None, None]
    total = [None, None]
    acc = [None, None]
    top[0] = score(0)
    top[1] = score(1)

    pltpu.make_async_copy(hrecv.at[pl.ds(0, REPS - 1)], hrecv.at[pl.ds(0, REPS - 1)], small_recv.at[0]).wait()
    for r in range(REPS):
        hall[pl.ds(r * TOKENS, TOKENS), :] = hrecv[r].astype(F32)
    product = jnp.dot(hall[...].astype(BF16), pooled[rep], preferred_element_type=F32)
    for r in range(REPS):
        psend[r] = product[r * TOKENS : (r + 1) * TOKENS, :]
    for k in range(1, REPS):
        peer = lax.rem(rep + k, REPS)
        small(psend.at[peer], precv.at[rep], 1, (peer, tp)).start()
    precv[rep] = psend[rep]

    total[0], acc[0] = weigh(0, top[0])
    event(1)
    event(2)
    event(3)
    total[1], acc[1] = weigh(1, top[1])
    event(4)
    event(5)

    pltpu.make_async_copy(precv.at[pl.ds(0, REPS - 1)], precv.at[pl.ds(0, REPS - 1)], small_recv.at[1]).wait()
    projected = precv[0]
    for r in range(1, REPS):
        projected = projected + precv[r]
    row = lax.broadcasted_iota(jnp.int32, (TOKENS, HEAD_DIM), 0)
    lane = lax.broadcasted_iota(jnp.int32, (TOKENS, HEAD_DIM), 1)
    position = jnp.where(row % 2 == 0, length[0], length[1]) + row // 2
    angle = position.astype(F32) * frequencies((TOKENS, HEAD_DIM))
    raw = projected[:, :HEAD_DIM]
    swapped = jnp.concatenate([raw[:, HEAD_DIM // 2 :], raw[:, : HEAD_DIM // 2]], axis=1)
    sine = jnp.where(lane < HEAD_DIM // 2, -jnp.sin(angle), jnp.sin(angle))
    new_keys = (raw * jnp.cos(angle) + swapped * sine).astype(BF16)
    new_values = projected[:, HEAD_DIM:].astype(BF16)
    for t in range(STEPS):
        appended[t, :, pl.ds(0, HEAD_DIM)] = new_keys[t * SESSIONS : (t + 1) * SESSIONS, :]
        appended[t, :, pl.ds(HEAD_DIM, HEAD_DIM)] = new_values[t * SESSIONS : (t + 1) * SESSIONS, :]
    new_keys = new_keys.astype(F32)
    new_values = new_values.astype(F32)
    second = lax.broadcasted_iota(jnp.int32, (QROWS, 1), 0) >= GROUP
    for s in range(SESSIONS):
        q = qrows[s]
        fresh = [
            jnp.sum(q * new_keys[u * SESSIONS + s : u * SESSIONS + s + 1, :], axis=1, keepdims=True) * SCALE
            for u in range(STEPS)]
        fresh[1] = jnp.where(second, fresh[1], -jnp.inf)
        peak = jnp.maximum(top[s], jnp.maximum(fresh[0], fresh[1]))
        keep = jnp.exp(top[s] - peak)
        fresh = [jnp.exp(x - peak) for x in fresh]
        whole = total[s] * keep + fresh[0] + fresh[1]
        out = acc[s] * (keep / whole)
        for u in range(STEPS):
            out = out + (fresh[u] / whole).astype(BF16).astype(F32) * new_values[u * SESSIONS + s : u * SESSIONS + s + 1, :]
        heads[s] = out
    lhs[...] = jnp.zeros(lhs.shape, F32)
    for s in range(SESSIONS):
        for t in range(STEPS):
            for q in range(GROUP):
                lhs[pl.ds(t * SESSIONS + s, 1), pl.ds(q * HEAD_DIM, HEAD_DIM)] = heads[s, pl.ds(t * GROUP + q, 1), :]
    left = lhs[...].astype(BF16)
    loads[9].wait()
    for k in range(1, TPS + 1):
        peer = lax.rem(tp + k, TPS)
        columns = pl.ds(pl.multiple_of(peer * OUT_COLS, OUT_COLS), OUT_COLS)
        part = jnp.dot(left, wbuf[:, columns], preferred_element_type=F32)[:TOKENS]
        if k == TPS:
            rrecv[tp] = part
        else:
            rsend[k] = part
            small(rsend.at[k], rrecv.at[tp], 2, (rep, peer)).start()
    event(6)
    event(7)
    event(8)
    event(9)
    event(14)

    pltpu.make_async_copy(rrecv.at[pl.ds(0, TPS - 1)], rrecv.at[pl.ds(0, TPS - 1)], small_recv.at[2]).wait()
    summed = rrecv[0]
    for r in range(1, TPS):
        summed = summed + rrecv[r]
    summed = summed.astype(BF16)
    mine = pl.ds(pl.multiple_of(tp * OUT_COLS, OUT_COLS), OUT_COLS)
    for t in range(STEPS):
        gsend[t] = summed[t * SESSIONS : (t + 1) * SESSIONS, :]
        attended[t, :, mine] = summed[t * SESSIONS : (t + 1) * SESSIONS, :]
    for k in range(1, TPS):
        small(gsend, attended.at[:, :, mine], 3, (rep, lax.rem(tp + k, TPS))).start()

    for n in (15, 16, 10, 11, 17, 18, 12, 13):
        event(n)

    def drain(ref, sem):
        pltpu.make_async_copy(ref, ref, sem).wait()

    others = attended.at[:, :, pl.ds(0, (TPS - 1) * OUT_COLS)]
    drain(others, small_recv.at[3])
    drain(pooled.at[pl.ds(0, REPS // 2)], sib_recv)
    drain(pooled.at[pl.ds(0, REPS - 1)], bulk_send)
    drain(hsend.at[pl.ds(0, REPS - 1)], small_send.at[0])
    drain(psend.at[pl.ds(0, REPS - 1)], small_send.at[1])
    drain(rsend.at[pl.ds(0, TPS - 1)], small_send.at[2])
    drain(others, small_send.at[3])


def write_kernel(owners, pooled, attended, appended, installed, attended_out, appended_out, sem):
    copies = [
        pltpu.make_async_copy(pooled.at[owners[s]], installed.at[s], sem.at[s]) for s in range(REPS)]
    copies.append(pltpu.make_async_copy(attended, attended_out, sem.at[REPS]))
    copies.append(pltpu.make_async_copy(appended, appended_out, sem.at[REPS + 1]))
    for copy in copies:
        copy.start()
    for copy in copies:
        copy.wait()


def shards(hidden, queries, sectioned, owners, keys, values, lengths, weight):
    hbm = pl.BlockSpec(memory_space=pltpu.HBM)
    vmem = pl.BlockSpec(memory_space=pltpu.VMEM)
    pooled, attended, appended = pl.pallas_call(
        main_kernel,
        out_shape=(
            pltpu.VMEM((REPS, ROWS, COLS), BF16),
            pltpu.VMEM((STEPS, SESSIONS, TPS * OUT_COLS), BF16),
            pltpu.VMEM((STEPS, SESSIONS, COLS), BF16),
        ),
        in_specs=[hbm] * 8,
        out_specs=(vmem, vmem, vmem),
        scratch_shapes=[
            pltpu.VMEM((SESSIONS, SLOTS, HEAD_DIM), BF16),
            pltpu.VMEM((SESSIONS, SLOTS, HEAD_DIM), BF16),
            pltpu.VMEM((GROUP * HEAD_DIM, TPS * OUT_COLS), BF16),
            pltpu.VMEM((STEPS, SESSIONS, REPS * ROWS), BF16),
            pltpu.VMEM((STEPS, SESSIONS, GROUP * HEAD_DIM), BF16),
            pltpu.SMEM((REPS,), jnp.int32),
            pltpu.SMEM((SESSIONS,), jnp.int32),
            pltpu.VMEM((REPS, TOKENS, ROWS), F32),
            pltpu.VMEM((REPS, TOKENS, ROWS), BF16),
            pltpu.VMEM((REPS, TOKENS, ROWS), BF16),
            pltpu.VMEM((REPS * TOKENS, ROWS), F32),
            pltpu.VMEM((REPS, TOKENS, COLS), F32),
            pltpu.VMEM((REPS, TOKENS, COLS), F32),
            pltpu.VMEM((SESSIONS, QROWS, HEAD_DIM), F32),
            pltpu.VMEM((SESSIONS, QROWS, SLOTS), F32),
            pltpu.VMEM((SESSIONS, QROWS, HEAD_DIM), F32),
            pltpu.VMEM((8, GROUP * HEAD_DIM), F32),
            pltpu.VMEM((TPS, TOKENS, OUT_COLS), F32),
            pltpu.VMEM((TPS, TOKENS, OUT_COLS), F32),
            pltpu.VMEM((STEPS, SESSIONS, OUT_COLS), BF16),
            pltpu.SemaphoreType.DMA((10,)),
            pltpu.SemaphoreType.DMA,
            pltpu.SemaphoreType.DMA((19,)),
            pltpu.SemaphoreType.DMA,
            pltpu.SemaphoreType.DMA((4,)),
            pltpu.SemaphoreType.DMA((4,)),
        ],
        compiler_params=pltpu.CompilerParams(
            collective_id=0, has_side_effects=True, vmem_limit_bytes=32 << 20),
        name="gather_and_attend",
    )(hidden, queries, sectioned, owners, keys, values, lengths, weight)
    installed, attended, appended = pl.pallas_call(
        write_kernel,
        out_shape=(
            jax.ShapeDtypeStruct((REPS, ROWS, COLS), BF16),
            jax.ShapeDtypeStruct(attended.shape, BF16),
            jax.ShapeDtypeStruct(appended.shape, BF16),
        ),
        grid_spec=pltpu.PrefetchScalarGridSpec(
            num_scalar_prefetch=1,
            grid=(),
            in_specs=[vmem, vmem, vmem],
            out_specs=(hbm, hbm, hbm),
            scratch_shapes=[pltpu.SemaphoreType.DMA((REPS + 2,))],
        ),
        compiler_params=pltpu.CompilerParams(vmem_limit_bytes=4 << 20),
        name="write_in_order",
    )(owners, pooled, attended, appended)
    return installed.reshape(REPS * ROWS, COLS), appended, attended


def solution(mesh):
    in_specs = (
        P(None, "rep", None),
        P(None, "rep", "tp"),
        P("rep", "tp"),
        P(),
        P("rep", None, "tp"),
        P("rep", None, "tp"),
        P("rep"),
        P("tp", None),
    )
    out_specs = (P(None, "tp"), P(None, "rep", "tp"), P(None, "rep", None))
    return jax.shard_map(shards, mesh=mesh, in_specs=in_specs, out_specs=out_specs, check_vma=False)
```

```python
import functools
import math

import jax
import jax.numpy as jnp
from jax import lax
from jax.experimental import pallas as pl
from jax.experimental.pallas import tpu as pltpu
from jax.sharding import PartitionSpec as P

HEAD_DIM = 128
ROPE_BASE = 500000.0
SCALE = HEAD_DIM**-0.5
MESH = pl.DeviceIdType.MESH
F32 = jnp.float32
BF16 = jnp.bfloat16

REPS = 16
TPS = 8
ROWS = 512
COLS = 256
STEPS = 2
SESSIONS = 2
TOKENS = STEPS * SESSIONS
GROUP = 8
QROWS = STEPS * GROUP
SLOTS = 8192
CHUNK = 2048
OUT_COLS = 512
HALF = 2048

A0 = (0, 160)
A1 = (160, 176)
A = (0, 336)
B0 = (336, 80)
B1 = (416, 96)
B = (336, 176)
WHOLE = (0, 512)


def frequencies(shape):
    lane = lax.broadcasted_iota(jnp.int32, shape, 1) % (HEAD_DIM // 2)
    result = jnp.ones(shape, F32)
    for bit in range(6):
        factor = math.exp(-math.log(ROPE_BASE) * (1 << bit) / (HEAD_DIM // 2))
        result = result * jnp.where((lane // (1 << bit)) % 2 == 1, factor, 1.0).astype(F32)
    return result


def main_kernel(
    hidden, queries, sectioned, owners, keys, values, lengths, weight,
    pooled, attended, appended,
    kbuf, vbuf, wbuf, hbuf, qbuf, own_s, len_s, hsplit, hsend, hrecv, hall, psend, precv,
    qrows, scores, heads, lhs, osend, orecv,
    load_sem, bulk_send, bulk_recv, sib_recv, small_send, small_recv, ready,
):
    rep = lax.axis_index("rep")
    tp = lax.axis_index("tp")
    y, z, c = rep // 8, (rep // 2) % 4, rep % 2

    def chip(yy, zz, cc):
        return yy * 8 + lax.rem(zz + 4, 4) * 2 + cc

    zp = (chip(y, z + 1, c), tp)
    zm = (chip(y, z - 1, c), tp)
    yn = (chip(1 - y, z, c), tp)
    sib = (chip(y, z, 1 - c), tp)

    loads = [
        pltpu.make_async_copy(owners, own_s, load_sem.at[0]),
        pltpu.make_async_copy(hidden, hbuf, load_sem.at[1]),
        pltpu.make_async_copy(sectioned, pooled.at[rep], load_sem.at[2]),
        pltpu.make_async_copy(lengths, len_s, load_sem.at[3]),
        pltpu.make_async_copy(queries, qbuf, load_sem.at[4]),
        pltpu.make_async_copy(keys.at[0], kbuf.at[0], load_sem.at[5]),
        pltpu.make_async_copy(keys.at[1], kbuf.at[1], load_sem.at[6]),
        pltpu.make_async_copy(values.at[0], vbuf.at[0], load_sem.at[7]),
        pltpu.make_async_copy(values.at[1], vbuf.at[1], load_sem.at[8]),
        pltpu.make_async_copy(weight, wbuf, load_sem.at[9]),
    ]
    for load in loads[:5]:
        load.start()

    barrier = pltpu.get_barrier_semaphore()

    @pl.loop(0, REPS)
    def _(k):
        @pl.when((k != rep) & (k != 1))
        def _():
            pl.semaphore_signal(barrier, inc=1, device_id=(k, tp), device_id_type=MESH)

    loads[0].wait()

    loads[1].wait()
    for r in range(REPS):
        for t in range(STEPS):
            hsplit[r, t] = hbuf[t, :, pl.ds(r * ROWS, ROWS)]

    @pl.loop(0, REPS)
    def _(r):
        found = jnp.int32(0)
        for s in range(1, REPS):
            found = jnp.where(own_s[s] == r, s, found)
        hsend[r] = hsplit[found]

    loads[2].wait()
    for load in loads[5:]:
        load.start()

    @pl.when(rep != 1)
    def _():
        pl.semaphore_wait(barrier, REPS - 1)

    @pl.when(rep == 0)
    def _():
        pl.semaphore_signal(ready, inc=1, device_id=(1, tp), device_id_type=MESH)

        @pl.loop(1, TPS)
        def _(k):
            pl.semaphore_signal(barrier, inc=1, device_id=(1, lax.rem(tp + k, TPS)), device_id_type=MESH)

    @pl.when(rep == 1)
    def _():
        pl.semaphore_wait(ready, 1)

    def small(src, dst, which, device):
        return pltpu.make_async_remote_copy(
            src_ref=src, dst_ref=dst, send_sem=small_send.at[which], recv_sem=small_recv.at[which],
            device_id=device, device_id_type=MESH)

    @pl.loop(1, REPS)
    def _(k):
        peer = lax.rem(rep + k, REPS)
        small(hsend.at[peer], hrecv.at[rep], 0, (peer, tp)).start()

    hrecv[rep] = hsend[rep]

    def piece(block, part):
        return pooled.at[block, pl.ds(*part), :]

    def send(block, part, device, slot):
        ref = piece(block, part)
        pltpu.make_async_remote_copy(
            src_ref=ref, dst_ref=ref, send_sem=bulk_send, recv_sem=bulk_recv.at[slot],
            device_id=device, device_id_type=MESH).start()

    def to_sibling(block, part):
        ref = piece(block, part)
        pltpu.make_async_remote_copy(
            src_ref=ref, dst_ref=ref, send_sem=bulk_send, recv_sem=sib_recv,
            device_id=sib, device_id_type=MESH).start()

    def arrived(block, part, slot):
        ref = piece(block, part)
        pltpu.make_async_copy(ref, ref, bulk_recv.at[slot]).wait()

    here = {
        0: chip(y, z, c), 1: chip(y, z + 1, c), -1: chip(y, z - 1, c), 2: chip(y, z + 2, c)}
    there = {
        0: chip(1 - y, z, c), 1: chip(1 - y, z + 1, c), -1: chip(1 - y, z - 1, c), 2: chip(1 - y, z + 2, c)}

    def along(base, block, first, second):
        send(block, first, zp, base)
        send(block, second, zm, base + 2)

    def along_rest(base, block, first, second):
        send(block, second, zp, base + 1)
        send(block, first, zm, base + 3)

    def first_piece(base, row, first, second, down):
        block, part = (row[-1], first) if down else (row[1], second)
        arrived(block, part, base if down else base + 2)
        send(block, part, zp if down else zm, base + (4 if down else 5))
        return block, part

    def second_piece(base, row, first, second, whole, down):
        block, part = (row[-1], second) if down else (row[1], first)
        arrived(block, part, base + (1 if down else 3))
        to_sibling(block, whole)
        return block, part

    def far_piece(base, first, second, row, down):
        block, part = (row[2], first) if down else (row[2], second)
        arrived(block, part, base + (4 if down else 5))
        to_sibling(block, part)
        return block, part

    def b_first(down):
        block, part = first_piece(0, here, B0, B1, down)
        send(block, part, yn, 21 if down else 22)

    def b_second(down):
        second_piece(0, here, B0, B1, B, down)

    def b_second_across():
        send(here[-1], B1, yn, 23)
        send(here[1], B0, yn, 24)

    def b_far(down):
        block, part = far_piece(0, B0, B1, here, down)
        send(block, part, yn, 25 if down else 26)

    def a_across(n):
        part = (A0, A1)[n]
        arrived(there[0], part, 18 + n)
        if n == 0:
            send(there[0], A0, zp, 12)
            send(there[0], A0, zm, 15)
        else:
            send(there[0], A1, zm, 14)
            send(there[0], A1, zp, 13)
            to_sibling(there[0], A)

    def b_across(n):
        block, part = [
            (there[0], B), (there[-1], B0), (there[1], B1), (there[-1], B1), (there[1], B0), (there[2], B0), (there[2], B1)][n]
        arrived(block, part, 20 + n)
        to_sibling(block, part)

    along(0, here[0], B0, B1)
    send(here[0], A0, yn, 18)
    along_rest(0, here[0], B0, B1)
    send(here[0], A1, yn, 19)
    along(6, here[0], A0, A1)
    to_sibling(here[0], WHOLE)

    loads[3].wait()
    length = [len_s[s] for s in range(SESSIONS)]
    loads[4].wait()
    for s in range(SESSIONS):
        for t in range(STEPS):
            for q in range(GROUP):
                qrows[s, pl.ds(t * GROUP + q, 1), :] = qbuf[t, pl.ds(s, 1), pl.ds(q * HEAD_DIM, HEAD_DIM)].astype(F32)

    def score(s):
        loads[5 + s].wait()
        q = qrows[s].astype(BF16)

        def body(i, largest):
            start = pl.multiple_of(i * CHUNK, CHUNK)
            part = lax.dot_general(
                q, kbuf[s, pl.ds(start, CHUNK), :], (((1,), (1,)), ((), ())), preferred_element_type=F32) * SCALE
            slot = lax.broadcasted_iota(jnp.int32, (QROWS, CHUNK), 1) + start
            part = jnp.where(slot < length[s], part, -jnp.inf)
            scores[s, :, pl.ds(start, CHUNK)] = part
            for j in range(CHUNK // HEAD_DIM):
                largest = jnp.maximum(largest, part[:, j * HEAD_DIM : (j + 1) * HEAD_DIM])
            return largest

        largest = lax.fori_loop(0, SLOTS // CHUNK, body, jnp.full((QROWS, HEAD_DIM), -jnp.inf, F32))
        return jnp.max(largest, axis=1, keepdims=True)

    def weigh(s, top):
        loads[7 + s].wait()

        def body(i, carry):
            total, acc = carry
            start = pl.multiple_of(i * CHUNK, CHUNK)
            p = jnp.exp(scores[s, :, pl.ds(start, CHUNK)] - top)
            for j in range(CHUNK // HEAD_DIM):
                total = total + p[:, j * HEAD_DIM : (j + 1) * HEAD_DIM]
            acc = acc + jnp.dot(p.astype(BF16), vbuf[s, pl.ds(start, CHUNK), :], preferred_element_type=F32)
            return total, acc

        zero = jnp.zeros((QROWS, HEAD_DIM), F32)
        total, acc = lax.fori_loop(0, SLOTS // CHUNK, body, (zero, zero))
        return jnp.sum(total, axis=1, keepdims=True), acc

    top = [None, None]
    total = [None, None]
    acc = [None, None]
    top[0] = score(0)
    top[1] = score(1)

    pltpu.make_async_copy(hrecv.at[pl.ds(0, REPS - 1)], hrecv.at[pl.ds(0, REPS - 1)], small_recv.at[0]).wait()
    for r in range(REPS):
        for t in range(STEPS):
            hall[pl.ds(r * TOKENS + t * SESSIONS, SESSIONS), :] = hrecv[r, t].astype(F32)
    product = jnp.dot(hall[...].astype(BF16), pooled[rep], preferred_element_type=F32)
    for r in range(REPS):
        psend[r] = product[r * TOKENS : (r + 1) * TOKENS, :]

    @pl.loop(1, REPS)
    def _(k):
        peer = lax.rem(rep + k, REPS)
        small(psend.at[peer], precv.at[rep], 1, (peer, tp)).start()

    precv[rep] = psend[rep]

    along_rest(6, here[0], A0, A1)
    send(here[0], B, yn, 20)
    b_first(True)
    b_first(False)
    a_across(0)
    b_second(True)
    b_second(False)
    a_across(1)
    total[0], acc[0] = weigh(0, top[0])
    first_piece(6, here, A0, A1, True)
    first_piece(6, here, A0, A1, False)
    total[1], acc[1] = weigh(1, top[1])

    pltpu.make_async_copy(precv.at[pl.ds(0, REPS - 1)], precv.at[pl.ds(0, REPS - 1)], small_recv.at[1]).wait()
    projected = precv[0]
    for r in range(1, REPS):
        projected = projected + precv[r]
    row = lax.broadcasted_iota(jnp.int32, (TOKENS, HEAD_DIM), 0)
    lane = lax.broadcasted_iota(jnp.int32, (TOKENS, HEAD_DIM), 1)
    position = jnp.where(row % 2 == 0, length[0], length[1]) + row // 2
    angle = position.astype(F32) * frequencies((TOKENS, HEAD_DIM))
    raw = projected[:, :HEAD_DIM]
    swapped = jnp.concatenate([raw[:, HEAD_DIM // 2 :], raw[:, : HEAD_DIM // 2]], axis=1)
    sine = jnp.where(lane < HEAD_DIM // 2, -jnp.sin(angle), jnp.sin(angle))
    new_keys = (raw * jnp.cos(angle) + swapped * sine).astype(BF16)
    new_values = projected[:, HEAD_DIM:].astype(BF16)
    for t in range(STEPS):
        appended[t, :, pl.ds(0, HEAD_DIM)] = new_keys[t * SESSIONS : (t + 1) * SESSIONS, :]
        appended[t, :, pl.ds(HEAD_DIM, HEAD_DIM)] = new_values[t * SESSIONS : (t + 1) * SESSIONS, :]
    new_keys = new_keys.astype(F32)
    new_values = new_values.astype(F32)
    second = lax.broadcasted_iota(jnp.int32, (QROWS, 1), 0) >= GROUP
    for s in range(SESSIONS):
        q = qrows[s]
        fresh = [
            jnp.sum(q * new_keys[u * SESSIONS + s : u * SESSIONS + s + 1, :], axis=1, keepdims=True) * SCALE
            for u in range(STEPS)]
        fresh[1] = jnp.where(second, fresh[1], -jnp.inf)
        peak = jnp.maximum(top[s], jnp.maximum(fresh[0], fresh[1]))
        keep = jnp.exp(top[s] - peak)
        fresh = [jnp.exp(x - peak) for x in fresh]
        whole = total[s] * keep + fresh[0] + fresh[1]
        out = acc[s] * (keep / whole)
        for u in range(STEPS):
            out = out + (fresh[u] / whole).astype(BF16).astype(F32) * new_values[u * SESSIONS + s : u * SESSIONS + s + 1, :]
        heads[s] = out
    lhs[...] = jnp.zeros(lhs.shape, F32)
    for s in range(SESSIONS):
        for t in range(STEPS):
            for q in range(GROUP):
                lhs[pl.ds(t * SESSIONS + s, 1), pl.ds(q * HEAD_DIM, HEAD_DIM)] = heads[s, pl.ds(t * GROUP + q, 1), :]
    left = lhs[...].astype(BF16)
    loads[9].wait()

    @pl.when(rep != 1)
    def _():
        pl.semaphore_wait(ready, 1)

    @pl.when(rep == 1)
    def _():
        pl.semaphore_wait(barrier, TPS - 1)

        @pl.loop(0, REPS)
        def _(k):
            @pl.when(k != 1)
            def _():
                pl.semaphore_signal(ready, inc=1, device_id=(k, tp), device_id_type=MESH)

    for half in range(2):
        @pl.loop(0, HALF // OUT_COLS)
        def _(i):
            start = pl.multiple_of(i * OUT_COLS, OUT_COLS)
            part = jnp.dot(left, wbuf[:, pl.ds(half * HALF + start, OUT_COLS)], preferred_element_type=F32)
            osend[half, :, pl.ds(start, OUT_COLS)] = part[:TOKENS].astype(BF16)

        @pl.loop(1, TPS)
        def _(k):
            small(osend.at[half], orecv.at[half, tp], 2, (rep, lax.rem(tp + k, TPS))).start()

    b_second_across()
    second_piece(6, here, A0, A1, A, True)
    second_piece(6, here, A0, A1, A, False)
    b_across(0)
    b_far(True)
    b_far(False)
    b_across(1)
    b_across(2)
    first_piece(12, there, A0, A1, True)
    first_piece(12, there, A0, A1, False)
    b_across(3)
    second_piece(12, there, A0, A1, A, True)
    second_piece(12, there, A0, A1, A, False)
    b_across(4)
    far_piece(6, A0, A1, here, True)
    far_piece(6, A0, A1, here, False)
    b_across(5)
    b_across(6)
    far_piece(12, A0, A1, there, True)
    far_piece(12, A0, A1, there, False)

    def drain(ref, sem):
        pltpu.make_async_copy(ref, ref, sem).wait()

    others = orecv.at[:, pl.ds(0, TPS - 1)]
    drain(others, small_recv.at[2])
    for half in range(2):
        orecv[half, tp] = osend[half]
        for i in range(HALF // OUT_COLS):
            columns = pl.ds(i * OUT_COLS, OUT_COLS)
            summed = orecv[half, 0, :, columns].astype(F32)
            for r in range(1, TPS):
                summed = summed + orecv[half, r, :, columns].astype(F32)
            summed = summed.astype(BF16)
            for t in range(STEPS):
                attended[t, :, pl.ds(half * HALF + i * OUT_COLS, OUT_COLS)] = summed[t * SESSIONS : (t + 1) * SESSIONS, :]

    drain(pooled.at[pl.ds(0, REPS // 2)], sib_recv)
    drain(pooled.at[pl.ds(0, REPS - 1)], bulk_send)
    drain(hsend.at[pl.ds(0, REPS - 1)], small_send.at[0])
    drain(psend.at[pl.ds(0, REPS - 1)], small_send.at[1])
    drain(others, small_send.at[2])


def write_kernel(owners, pooled, attended, appended, installed, attended_out, appended_out, sem):
    copies = [
        pltpu.make_async_copy(pooled.at[owners[s]], installed.at[s], sem.at[s]) for s in range(REPS)]
    copies.append(pltpu.make_async_copy(attended, attended_out, sem.at[REPS]))
    copies.append(pltpu.make_async_copy(appended, appended_out, sem.at[REPS + 1]))
    for copy in copies:
        copy.start()
    for copy in copies:
        copy.wait()


def shards(hidden, queries, sectioned, owners, keys, values, lengths, weight):
    operands = [
        pltpu.with_memory_space_constraint(x, pltpu.HBM)
        for x in (hidden, queries, sectioned, owners, keys, values, lengths, weight)]
    hbm = pl.BlockSpec(memory_space=pltpu.HBM)
    vmem = pl.BlockSpec(memory_space=pltpu.VMEM)
    pooled, attended, appended = pl.pallas_call(
        main_kernel,
        out_shape=(
            pltpu.VMEM((REPS, ROWS, COLS), BF16),
            pltpu.VMEM((STEPS, SESSIONS, 2 * HALF), BF16),
            pltpu.VMEM((STEPS, SESSIONS, COLS), BF16),
        ),
        in_specs=[hbm] * 8,
        out_specs=(vmem, vmem, vmem),
        scratch_shapes=[
            pltpu.VMEM((SESSIONS, SLOTS, HEAD_DIM), BF16),
            pltpu.VMEM((SESSIONS, SLOTS, HEAD_DIM), BF16),
            pltpu.VMEM((GROUP * HEAD_DIM, 2 * HALF), BF16),
            pltpu.VMEM((STEPS, SESSIONS, REPS * ROWS), BF16),
            pltpu.VMEM((STEPS, SESSIONS, GROUP * HEAD_DIM), BF16),
            pltpu.SMEM((REPS,), jnp.int32),
            pltpu.SMEM((SESSIONS,), jnp.int32),
            pltpu.VMEM((REPS, STEPS, SESSIONS, ROWS), BF16),
            pltpu.VMEM((REPS, STEPS, SESSIONS, ROWS), BF16),
            pltpu.VMEM((REPS, STEPS, SESSIONS, ROWS), BF16),
            pltpu.VMEM((REPS * TOKENS, ROWS), F32),
            pltpu.VMEM((REPS, TOKENS, COLS), F32),
            pltpu.VMEM((REPS, TOKENS, COLS), F32),
            pltpu.VMEM((SESSIONS, QROWS, HEAD_DIM), F32),
            pltpu.VMEM((SESSIONS, QROWS, SLOTS), F32),
            pltpu.VMEM((SESSIONS, QROWS, HEAD_DIM), F32),
            pltpu.VMEM((8, GROUP * HEAD_DIM), F32),
            pltpu.VMEM((2, TOKENS, HALF), BF16),
            pltpu.VMEM((2, TPS, TOKENS, HALF), BF16),
            pltpu.SemaphoreType.DMA((10,)),
            pltpu.SemaphoreType.DMA,
            pltpu.SemaphoreType.DMA((27,)),
            pltpu.SemaphoreType.DMA,
            pltpu.SemaphoreType.DMA((3,)),
            pltpu.SemaphoreType.DMA((3,)),
            pltpu.SemaphoreType.REGULAR,
        ],
        compiler_params=pltpu.CompilerParams(
            collective_id=0, has_side_effects=True, vmem_limit_bytes=32 << 20),
        name="gather_and_attend",
    )(*operands)
    installed, attended, appended = pl.pallas_call(
        write_kernel,
        out_shape=(
            jax.ShapeDtypeStruct((REPS, ROWS, COLS), BF16),
            jax.ShapeDtypeStruct(attended.shape, BF16),
            jax.ShapeDtypeStruct(appended.shape, BF16),
        ),
        grid_spec=pltpu.PrefetchScalarGridSpec(
            num_scalar_prefetch=1,
            grid=(),
            in_specs=[vmem, vmem, vmem],
            out_specs=(hbm, hbm, hbm),
            scratch_shapes=[pltpu.SemaphoreType.DMA((REPS + 2,))],
        ),
        compiler_params=pltpu.CompilerParams(vmem_limit_bytes=4 << 20),
        name="write_in_order",
    )(owners, pooled, attended, appended)
    return installed.reshape(REPS * ROWS, COLS), appended, attended


def solution(mesh):
    in_specs = (
        P(None, "rep", None),
        P(None, "rep", "tp"),
        P("rep", "tp"),
        P(),
        P("rep", None, "tp"),
        P("rep", None, "tp"),
        P("rep"),
        P("tp", None),
    )
    out_specs = (P(None, "tp"), P(None, "rep", "tp"), P(None, "rep", None))
    return jax.shard_map(shards, mesh=mesh, in_specs=in_specs, out_specs=out_specs, check_vma=False)
```

```python
import functools
import math

import jax
import jax.numpy as jnp
from jax import lax
from jax.experimental import pallas as pl
from jax.experimental.pallas import tpu as pltpu
from jax.sharding import PartitionSpec as P

HEAD_DIM = 128
ROPE_BASE = 500000.0
SCALE = HEAD_DIM**-0.5
MESH = pl.DeviceIdType.MESH
F32 = jnp.float32
BF16 = jnp.bfloat16

REPS = 16
TPS = 8
ROWS = 512
COLS = 256
STEPS = 2
SESSIONS = 2
TOKENS = STEPS * SESSIONS
GROUP = 8
QROWS = STEPS * GROUP
SLOTS = 8192
CHUNK = 2048
OUT_COLS = 512
HALF = 2048

A0 = (0, 160)
A1 = (160, 176)
A = (0, 336)
B0 = (336, 80)
B1 = (416, 96)
B = (336, 176)
WHOLE = (0, 512)


def frequencies(shape):
    lane = lax.broadcasted_iota(jnp.int32, shape, 1) % (HEAD_DIM // 2)
    result = jnp.ones(shape, F32)
    for bit in range(6):
        factor = math.exp(-math.log(ROPE_BASE) * (1 << bit) / (HEAD_DIM // 2))
        result = result * jnp.where((lane // (1 << bit)) % 2 == 1, factor, 1.0).astype(F32)
    return result


def main_kernel(
    hidden, queries, sectioned, owners, keys, values, lengths, weight,
    pooled, attended, appended,
    kbuf, vbuf, wbuf, hbuf, qbuf, own_s, len_s, hsplit, hsend, hrecv, hall, psend, precv,
    qrows, scores, heads, lhs, osend, orecv,
    load_sem, bulk_send, bulk_recv, sib_recv, small_send, small_recv, ready,
):
    rep = lax.axis_index("rep")
    tp = lax.axis_index("tp")
    y, z, c = rep // 8, (rep // 2) % 4, rep % 2

    def chip(yy, zz, cc):
        return yy * 8 + lax.rem(zz + 4, 4) * 2 + cc

    zp = (chip(y, z + 1, c), tp)
    zm = (chip(y, z - 1, c), tp)
    yn = (chip(1 - y, z, c), tp)
    sib = (chip(y, z, 1 - c), tp)

    loads = [
        pltpu.make_async_copy(owners, own_s, load_sem.at[0]),
        pltpu.make_async_copy(hidden, hbuf, load_sem.at[1]),
        pltpu.make_async_copy(sectioned, pooled.at[rep], load_sem.at[2]),
        pltpu.make_async_copy(lengths, len_s, load_sem.at[3]),
        pltpu.make_async_copy(queries, qbuf, load_sem.at[4]),
        pltpu.make_async_copy(keys.at[0], kbuf.at[0], load_sem.at[5]),
        pltpu.make_async_copy(keys.at[1], kbuf.at[1], load_sem.at[6]),
        pltpu.make_async_copy(values.at[0], vbuf.at[0], load_sem.at[7]),
        pltpu.make_async_copy(values.at[1], vbuf.at[1], load_sem.at[8]),
        pltpu.make_async_copy(weight, wbuf, load_sem.at[9]),
    ]
    for load in loads[:5]:
        load.start()

    barrier = pltpu.get_barrier_semaphore()

    @pl.loop(0, REPS)
    def _(k):
        @pl.when((k != rep) & (k != 1))
        def _():
            pl.semaphore_signal(barrier, inc=1, device_id=(k, tp), device_id_type=MESH)

    loads[0].wait()

    loads[1].wait()
    for r in range(REPS):
        for t in range(STEPS):
            hsplit[r, t] = hbuf[t, :, pl.ds(r * ROWS, ROWS)]

    @pl.loop(0, REPS)
    def _(r):
        found = jnp.int32(0)
        for s in range(1, REPS):
            found = jnp.where(own_s[s] == r, s, found)
        hsend[r] = hsplit[found]

    loads[2].wait()
    for load in loads[5:]:
        load.start()

    @pl.when(rep != 1)
    def _():
        pl.semaphore_wait(barrier, REPS - 1)

    @pl.when(rep == 0)
    def _():
        pl.semaphore_signal(ready, inc=1, device_id=(1, tp), device_id_type=MESH)

        @pl.loop(1, TPS)
        def _(k):
            pl.semaphore_signal(barrier, inc=1, device_id=(1, lax.rem(tp + k, TPS)), device_id_type=MESH)

    @pl.when(rep == 1)
    def _():
        pl.semaphore_wait(ready, 1)

    def small(src, dst, which, device):
        return pltpu.make_async_remote_copy(
            src_ref=src, dst_ref=dst, send_sem=small_send.at[which], recv_sem=small_recv.at[which],
            device_id=device, device_id_type=MESH)

    @pl.loop(1, REPS)
    def _(k):
        peer = lax.rem(rep + k, REPS)
        small(hsend.at[peer], hrecv.at[rep], 0, (peer, tp)).start()

    hrecv[rep] = hsend[rep]

    def piece(block, part):
        return pooled.at[block, pl.ds(*part), :]

    def send(block, part, device, slot):
        ref = piece(block, part)
        pltpu.make_async_remote_copy(
            src_ref=ref, dst_ref=ref, send_sem=bulk_send, recv_sem=bulk_recv.at[slot],
            device_id=device, device_id_type=MESH).start()

    def to_sibling(block, part):
        ref = piece(block, part)
        pltpu.make_async_remote_copy(
            src_ref=ref, dst_ref=ref, send_sem=bulk_send, recv_sem=sib_recv,
            device_id=sib, device_id_type=MESH).start()

    def arrived(block, part, slot):
        ref = piece(block, part)
        pltpu.make_async_copy(ref, ref, bulk_recv.at[slot]).wait()

    here = {
        0: chip(y, z, c), 1: chip(y, z + 1, c), -1: chip(y, z - 1, c), 2: chip(y, z + 2, c)}
    there = {
        0: chip(1 - y, z, c), 1: chip(1 - y, z + 1, c), -1: chip(1 - y, z - 1, c), 2: chip(1 - y, z + 2, c)}

    route = [
        (here[-1], B, [(zp, B0, 5), (yn, B, 7)]),
        (here[1], B, [(zm, B1, 6), (yn, B, 8)]),
        (there[0], A, [(zp, A, 11), (zm, A, 12)]),
        (here[-1], A, [(zp, A0, 13)]),
        (here[1], A, [(zm, A1, 14)]),
        (here[2], B0, [(yn, B0, 9)]),
        (here[2], B1, [(yn, B1, 10)]),
        (there[-1], B, []),
        (there[1], B, []),
        (there[2], B0, []),
        (there[2], B1, []),
        (there[-1], A, [(zp, A0, 15)]),
        (there[1], A, [(zm, A1, 16)]),
        (here[2], A0, []),
        (here[2], A1, []),
        (there[2], A0, []),
        (there[2], A1, []),
        (there[0], B, []),
    ]

    def events(*slots):
        for n in slots:
            block, part, onward = route[n]
            arrived(block, part, n)
            for device, onward_part, slot in onward:
                send(block, onward_part, device, slot)
        done = [(route[n][0], route[n][1]) for n in slots]
        if len(done) == 2 and done[0][0] is done[1][0]:
            to_sibling(done[0][0], (done[0][1][0], done[0][1][1] + done[1][1][1]))
        else:
            for block, part in done:
                to_sibling(block, part)

    send(here[0], B, zp, 0)
    send(here[0], B, zm, 1)
    send(here[0], A, yn, 2)
    send(here[0], A, zp, 3)
    send(here[0], A, zm, 4)
    send(here[0], B, yn, 17)
    to_sibling(here[0], WHOLE)

    loads[3].wait()
    length = [len_s[s] for s in range(SESSIONS)]
    loads[4].wait()
    for s in range(SESSIONS):
        for t in range(STEPS):
            for q in range(GROUP):
                qrows[s, pl.ds(t * GROUP + q, 1), :] = qbuf[t, pl.ds(s, 1), pl.ds(q * HEAD_DIM, HEAD_DIM)].astype(F32)

    def score(s):
        loads[5 + s].wait()
        q = qrows[s].astype(BF16)

        def body(i, largest):
            start = pl.multiple_of(i * CHUNK, CHUNK)
            part = lax.dot_general(
                q, kbuf[s, pl.ds(start, CHUNK), :], (((1,), (1,)), ((), ())), preferred_element_type=F32) * SCALE
            slot = lax.broadcasted_iota(jnp.int32, (QROWS, CHUNK), 1) + start
            part = jnp.where(slot < length[s], part, -jnp.inf)
            scores[s, :, pl.ds(start, CHUNK)] = part
            for j in range(CHUNK // HEAD_DIM):
                largest = jnp.maximum(largest, part[:, j * HEAD_DIM : (j + 1) * HEAD_DIM])
            return largest

        largest = lax.fori_loop(0, SLOTS // CHUNK, body, jnp.full((QROWS, HEAD_DIM), -jnp.inf, F32))
        return jnp.max(largest, axis=1, keepdims=True)

    def weigh(s, top):
        loads[7 + s].wait()

        def body(i, carry):
            total, acc = carry
            start = pl.multiple_of(i * CHUNK, CHUNK)
            p = jnp.exp(scores[s, :, pl.ds(start, CHUNK)] - top)
            for j in range(CHUNK // HEAD_DIM):
                total = total + p[:, j * HEAD_DIM : (j + 1) * HEAD_DIM]
            acc = acc + jnp.dot(p.astype(BF16), vbuf[s, pl.ds(start, CHUNK), :], preferred_element_type=F32)
            return total, acc

        zero = jnp.zeros((QROWS, HEAD_DIM), F32)
        total, acc = lax.fori_loop(0, SLOTS // CHUNK, body, (zero, zero))
        return jnp.sum(total, axis=1, keepdims=True), acc

    top = [None, None]
    total = [None, None]
    acc = [None, None]
    top[0] = score(0)
    top[1] = score(1)

    pltpu.make_async_copy(hrecv.at[pl.ds(0, REPS - 1)], hrecv.at[pl.ds(0, REPS - 1)], small_recv.at[0]).wait()
    for r in range(REPS):
        for t in range(STEPS):
            hall[pl.ds(r * TOKENS + t * SESSIONS, SESSIONS), :] = hrecv[r, t].astype(F32)
    product = jnp.dot(hall[...].astype(BF16), pooled[rep], preferred_element_type=F32)
    for r in range(REPS):
        psend[r] = product[r * TOKENS : (r + 1) * TOKENS, :]

    @pl.loop(1, REPS)
    def _(k):
        peer = lax.rem(rep + k, REPS)
        small(psend.at[peer], precv.at[rep], 1, (peer, tp)).start()

    precv[rep] = psend[rep]

    events(0, 1)
    events(2)
    total[0], acc[0] = weigh(0, top[0])
    total[1], acc[1] = weigh(1, top[1])
    events(3, 4)
    events(5, 6)

    pltpu.make_async_copy(precv.at[pl.ds(0, REPS - 1)], precv.at[pl.ds(0, REPS - 1)], small_recv.at[1]).wait()
    projected = precv[0]
    for r in range(1, REPS):
        projected = projected + precv[r]
    row = lax.broadcasted_iota(jnp.int32, (TOKENS, HEAD_DIM), 0)
    lane = lax.broadcasted_iota(jnp.int32, (TOKENS, HEAD_DIM), 1)
    position = jnp.where(row % 2 == 0, length[0], length[1]) + row // 2
    angle = position.astype(F32) * frequencies((TOKENS, HEAD_DIM))
    raw = projected[:, :HEAD_DIM]
    swapped = jnp.concatenate([raw[:, HEAD_DIM // 2 :], raw[:, : HEAD_DIM // 2]], axis=1)
    sine = jnp.where(lane < HEAD_DIM // 2, -jnp.sin(angle), jnp.sin(angle))
    new_keys = (raw * jnp.cos(angle) + swapped * sine).astype(BF16)
    new_values = projected[:, HEAD_DIM:].astype(BF16)
    for t in range(STEPS):
        appended[t, :, pl.ds(0, HEAD_DIM)] = new_keys[t * SESSIONS : (t + 1) * SESSIONS, :]
        appended[t, :, pl.ds(HEAD_DIM, HEAD_DIM)] = new_values[t * SESSIONS : (t + 1) * SESSIONS, :]
    new_keys = new_keys.astype(F32)
    new_values = new_values.astype(F32)
    second = lax.broadcasted_iota(jnp.int32, (QROWS, 1), 0) >= GROUP
    for s in range(SESSIONS):
        q = qrows[s]
        fresh = [
            jnp.sum(q * new_keys[u * SESSIONS + s : u * SESSIONS + s + 1, :], axis=1, keepdims=True) * SCALE
            for u in range(STEPS)]
        fresh[1] = jnp.where(second, fresh[1], -jnp.inf)
        peak = jnp.maximum(top[s], jnp.maximum(fresh[0], fresh[1]))
        keep = jnp.exp(top[s] - peak)
        fresh = [jnp.exp(x - peak) for x in fresh]
        whole = total[s] * keep + fresh[0] + fresh[1]
        out = acc[s] * (keep / whole)
        for u in range(STEPS):
            out = out + (fresh[u] / whole).astype(BF16).astype(F32) * new_values[u * SESSIONS + s : u * SESSIONS + s + 1, :]
        heads[s] = out
    lhs[...] = jnp.zeros(lhs.shape, F32)
    for s in range(SESSIONS):
        for t in range(STEPS):
            for q in range(GROUP):
                lhs[pl.ds(t * SESSIONS + s, 1), pl.ds(q * HEAD_DIM, HEAD_DIM)] = heads[s, pl.ds(t * GROUP + q, 1), :]
    left = lhs[...].astype(BF16)
    loads[9].wait()

    @pl.when(rep != 1)
    def _():
        pl.semaphore_wait(ready, 1)

    @pl.when(rep == 1)
    def _():
        pl.semaphore_wait(barrier, TPS - 1)

        @pl.loop(0, REPS)
        def _(k):
            @pl.when(k != 1)
            def _():
                pl.semaphore_signal(ready, inc=1, device_id=(k, tp), device_id_type=MESH)

    for half in range(2):
        @pl.loop(0, HALF // OUT_COLS)
        def _(i):
            start = pl.multiple_of(i * OUT_COLS, OUT_COLS)
            part = jnp.dot(left, wbuf[:, pl.ds(half * HALF + start, OUT_COLS)], preferred_element_type=F32)
            osend[half, :, pl.ds(start, OUT_COLS)] = part[:TOKENS].astype(BF16)

        @pl.loop(1, TPS)
        def _(k):
            small(osend.at[half], orecv.at[half, tp], 2, (rep, lax.rem(tp + k, TPS))).start()

    events(11, 12)
    events(17)
    events(7, 8)
    events(13, 14)
    events(9, 10)
    events(15, 16)

    def drain(ref, sem):
        pltpu.make_async_copy(ref, ref, sem).wait()

    others = orecv.at[:, pl.ds(0, TPS - 1)]
    drain(others, small_recv.at[2])
    for half in range(2):
        orecv[half, tp] = osend[half]
        for i in range(HALF // OUT_COLS):
            columns = pl.ds(i * OUT_COLS, OUT_COLS)
            summed = orecv[half, 0, :, columns].astype(F32)
            for r in range(1, TPS):
                summed = summed + orecv[half, r, :, columns].astype(F32)
            summed = summed.astype(BF16)
            for t in range(STEPS):
                attended[t, :, pl.ds(half * HALF + i * OUT_COLS, OUT_COLS)] = summed[t * SESSIONS : (t + 1) * SESSIONS, :]

    drain(pooled.at[pl.ds(0, REPS // 2)], sib_recv)
    drain(pooled.at[pl.ds(0, REPS - 1)], bulk_send)
    drain(hsend.at[pl.ds(0, REPS - 1)], small_send.at[0])
    drain(psend.at[pl.ds(0, REPS - 1)], small_send.at[1])
    drain(others, small_send.at[2])


def write_kernel(owners, pooled, attended, appended, installed, attended_out, appended_out, sem):
    copies = [
        pltpu.make_async_copy(pooled.at[owners[s]], installed.at[s], sem.at[s]) for s in range(REPS)]
    copies.append(pltpu.make_async_copy(attended, attended_out, sem.at[REPS]))
    copies.append(pltpu.make_async_copy(appended, appended_out, sem.at[REPS + 1]))
    for copy in copies:
        copy.start()
    for copy in copies:
        copy.wait()


def shards(hidden, queries, sectioned, owners, keys, values, lengths, weight):
    operands = [
        pltpu.with_memory_space_constraint(x, pltpu.HBM)
        for x in (hidden, queries, sectioned, owners, keys, values, lengths, weight)]
    hbm = pl.BlockSpec(memory_space=pltpu.HBM)
    vmem = pl.BlockSpec(memory_space=pltpu.VMEM)
    pooled, attended, appended = pl.pallas_call(
        main_kernel,
        out_shape=(
            pltpu.VMEM((REPS, ROWS, COLS), BF16),
            pltpu.VMEM((STEPS, SESSIONS, 2 * HALF), BF16),
            pltpu.VMEM((STEPS, SESSIONS, COLS), BF16),
        ),
        in_specs=[hbm] * 8,
        out_specs=(vmem, vmem, vmem),
        scratch_shapes=[
            pltpu.VMEM((SESSIONS, SLOTS, HEAD_DIM), BF16),
            pltpu.VMEM((SESSIONS, SLOTS, HEAD_DIM), BF16),
            pltpu.VMEM((GROUP * HEAD_DIM, 2 * HALF), BF16),
            pltpu.VMEM((STEPS, SESSIONS, REPS * ROWS), BF16),
            pltpu.VMEM((STEPS, SESSIONS, GROUP * HEAD_DIM), BF16),
            pltpu.SMEM((REPS,), jnp.int32),
            pltpu.SMEM((SESSIONS,), jnp.int32),
            pltpu.VMEM((REPS, STEPS, SESSIONS, ROWS), BF16),
            pltpu.VMEM((REPS, STEPS, SESSIONS, ROWS), BF16),
            pltpu.VMEM((REPS, STEPS, SESSIONS, ROWS), BF16),
            pltpu.VMEM((REPS * TOKENS, ROWS), F32),
            pltpu.VMEM((REPS, TOKENS, COLS), F32),
            pltpu.VMEM((REPS, TOKENS, COLS), F32),
            pltpu.VMEM((SESSIONS, QROWS, HEAD_DIM), F32),
            pltpu.VMEM((SESSIONS, QROWS, SLOTS), F32),
            pltpu.VMEM((SESSIONS, QROWS, HEAD_DIM), F32),
            pltpu.VMEM((8, GROUP * HEAD_DIM), F32),
            pltpu.VMEM((2, TOKENS, HALF), BF16),
            pltpu.VMEM((2, TPS, TOKENS, HALF), BF16),
            pltpu.SemaphoreType.DMA((10,)),
            pltpu.SemaphoreType.DMA,
            pltpu.SemaphoreType.DMA((18,)),
            pltpu.SemaphoreType.DMA,
            pltpu.SemaphoreType.DMA((3,)),
            pltpu.SemaphoreType.DMA((3,)),
            pltpu.SemaphoreType.REGULAR,
        ],
        compiler_params=pltpu.CompilerParams(
            collective_id=0, has_side_effects=True, vmem_limit_bytes=32 << 20),
        name="gather_and_attend",
    )(*operands)
    installed, attended, appended = pl.pallas_call(
        write_kernel,
        out_shape=(
            jax.ShapeDtypeStruct((REPS, ROWS, COLS), BF16),
            jax.ShapeDtypeStruct(attended.shape, BF16),
            jax.ShapeDtypeStruct(appended.shape, BF16),
        ),
        grid_spec=pltpu.PrefetchScalarGridSpec(
            num_scalar_prefetch=1,
            grid=(),
            in_specs=[vmem, vmem, vmem],
            out_specs=(hbm, hbm, hbm),
            scratch_shapes=[pltpu.SemaphoreType.DMA((REPS + 2,))],
        ),
        compiler_params=pltpu.CompilerParams(vmem_limit_bytes=4 << 20),
        name="write_in_order",
    )(owners, pooled, attended, appended)
    return installed.reshape(REPS * ROWS, COLS), appended, attended


def solution(mesh):
    in_specs = (
        P(None, "rep", None),
        P(None, "rep", "tp"),
        P("rep", "tp"),
        P(),
        P("rep", None, "tp"),
        P("rep", None, "tp"),
        P("rep"),
        P("tp", None),
    )
    out_specs = (P(None, "tp"), P(None, "rep", "tp"), P(None, "rep", None))
    return jax.shard_map(shards, mesh=mesh, in_specs=in_specs, out_specs=out_specs, check_vma=False)
```

```python
import functools
import math

import jax
import jax.numpy as jnp
from jax import lax
from jax.experimental import pallas as pl
from jax.experimental.pallas import tpu as pltpu
from jax.sharding import PartitionSpec as P

HEAD_DIM = 128
ROPE_BASE = 500000.0
SCALE = HEAD_DIM**-0.5
MESH = pl.DeviceIdType.MESH
F32 = jnp.float32
BF16 = jnp.bfloat16

REPS = 16
TPS = 8
ROWS = 512
COLS = 256
STEPS = 2
SESSIONS = 2
TOKENS = STEPS * SESSIONS
GROUP = 8
QROWS = STEPS * GROUP
SLOTS = 8192
CHUNK = 2048
OUT_COLS = 512
PARTS = 4
PART = 1024

A0 = (0, 176)
A1 = (176, 176)
A = (0, 352)
B0 = (352, 80)
B1 = (432, 80)
B = (352, 160)
A0_MOST, A0_END = (0, 112), (112, 64)
A1_MOST, A1_END = (176, 112), (288, 64)
WHOLE = (0, 512)


def frequencies(shape):
    lane = lax.broadcasted_iota(jnp.int32, shape, 1) % (HEAD_DIM // 2)
    result = jnp.ones(shape, F32)
    for bit in range(6):
        factor = math.exp(-math.log(ROPE_BASE) * (1 << bit) / (HEAD_DIM // 2))
        result = result * jnp.where((lane // (1 << bit)) % 2 == 1, factor, 1.0).astype(F32)
    return result


def main_kernel(
    hidden, queries, sectioned, owners, keys, values, lengths, weight,
    pooled, attended, appended,
    kbuf, vbuf, wbuf, hbuf, qbuf, own_s, len_s, hsplit, hsend, hrecv, hall, psend, precv,
    qrows, scores, heads, lhs, osend, orecv,
    load_sem, bulk_send, bulk_recv, sib_recv, small_send, small_recv, ready,
):
    rep = lax.axis_index("rep")
    tp = lax.axis_index("tp")
    y, z, c = rep // 8, (rep // 2) % 4, rep % 2

    def chip(yy, zz, cc):
        return yy * 8 + lax.rem(zz + 4, 4) * 2 + cc

    zp = (chip(y, z + 1, c), tp)
    zm = (chip(y, z - 1, c), tp)
    yn = (chip(1 - y, z, c), tp)
    sib = (chip(y, z, 1 - c), tp)
    zp_other = (chip(y, z + 1, 1 - c), tp)
    zm_other = (chip(y, z - 1, 1 - c), tp)
    far_other = chip(1 - y, z + 2, 1 - c)

    loads = [
        pltpu.make_async_copy(owners, own_s, load_sem.at[0]),
        pltpu.make_async_copy(hidden, hbuf, load_sem.at[1]),
        pltpu.make_async_copy(sectioned, pooled.at[rep], load_sem.at[2]),
        pltpu.make_async_copy(lengths, len_s, load_sem.at[3]),
        pltpu.make_async_copy(queries, qbuf, load_sem.at[4]),
        pltpu.make_async_copy(keys.at[0], kbuf.at[0], load_sem.at[5]),
        pltpu.make_async_copy(keys.at[1], kbuf.at[1], load_sem.at[6]),
        pltpu.make_async_copy(values.at[0], vbuf.at[0], load_sem.at[7]),
        pltpu.make_async_copy(values.at[1], vbuf.at[1], load_sem.at[8]),
        pltpu.make_async_copy(weight, wbuf, load_sem.at[9]),
    ]
    for load in loads[:5]:
        load.start()

    barrier = pltpu.get_barrier_semaphore()

    @pl.loop(0, REPS)
    def _(k):
        @pl.when((k != rep) & (k != 1))
        def _():
            pl.semaphore_signal(barrier, inc=1, device_id=(k, tp), device_id_type=MESH)

    loads[1].wait()
    for r in range(REPS):
        for t in range(STEPS):
            hsplit[r, t] = hbuf[t, :, pl.ds(r * ROWS, ROWS)]
    loads[0].wait()
    owner = [own_s[s] for s in range(REPS)]
    for r in range(REPS):
        found = jnp.int32(0)
        for s in range(1, REPS):
            found = jnp.where(owner[s] == r, s, found)
        hsend[r] = hsplit[found]

    loads[2].wait()
    for load in loads[5:]:
        load.start()

    @pl.when(rep != 1)
    def _():
        pl.semaphore_wait(barrier, REPS - 1)

    @pl.when(rep == 0)
    def _():
        pl.semaphore_signal(ready, inc=1, device_id=(1, tp), device_id_type=MESH)

    @pl.when(rep == 1)
    def _():
        pl.semaphore_wait(ready, 1)

    def small(src, dst, which, device):
        return pltpu.make_async_remote_copy(
            src_ref=src, dst_ref=dst, send_sem=small_send.at[which], recv_sem=small_recv.at[which],
            device_id=device, device_id_type=MESH)

    @pl.loop(1, REPS)
    def _(k):
        peer = lax.rem(rep + k, REPS)
        small(hsend.at[peer], hrecv.at[rep], 0, (peer, tp)).start()

    hrecv[rep] = hsend[rep]

    def piece(block, part):
        return pooled.at[block, pl.ds(*part), :]

    def send(block, part, device, slot):
        ref = piece(block, part)
        pltpu.make_async_remote_copy(
            src_ref=ref, dst_ref=ref, send_sem=bulk_send, recv_sem=bulk_recv.at[slot],
            device_id=device, device_id_type=MESH).start()

    def to_sibling(block, part):
        ref = piece(block, part)
        pltpu.make_async_remote_copy(
            src_ref=ref, dst_ref=ref, send_sem=bulk_send, recv_sem=sib_recv,
            device_id=sib, device_id_type=MESH).start()

    def arrived(block, part, slot):
        ref = piece(block, part)
        pltpu.make_async_copy(ref, ref, bulk_recv.at[slot]).wait()

    here = {
        0: chip(y, z, c), 1: chip(y, z + 1, c), -1: chip(y, z - 1, c), 2: chip(y, z + 2, c)}
    there = {
        0: chip(1 - y, z, c), 1: chip(1 - y, z + 1, c), -1: chip(1 - y, z - 1, c), 2: chip(1 - y, z + 2, c)}

    route = [
        (here[-1], B, [(zp, B0, 5), (yn, B, 7)]),
        (here[1], B, [(zm, B1, 6), (yn, B, 8)]),
        (there[0], A, [(zp, A, 11), (zm, A, 12)]),
        (here[-1], A, [(zp, A0, 13)]),
        (here[1], A, [(zm, A1, 14)]),
        (here[2], B0, [(yn, B0, 9)]),
        (here[2], B1, [(yn, B1, 10)]),
        (there[-1], B, []),
        (there[1], B, []),
        (there[2], B0, []),
        (there[2], B1, []),
        (there[-1], A, [(zp, A0_MOST, 15), (zp, A0_END, 18), (zp_other, A0_END, 19)]),
        (there[1], A, [(zm, A1_MOST, 16), (zm, A1_END, 20), (zm_other, A1_END, 21)]),
        (here[2], A0, []),
        (here[2], A1, []),
        (there[2], A0_MOST, []),
        (there[2], A1_MOST, []),
        (there[0], B, []),
    ]

    def events(*slots):
        for n in slots:
            block, part, onward = route[n]
            arrived(block, part, n)
            for device, onward_part, slot in onward:
                send(block, onward_part, device, slot)
        done = [(route[n][0], route[n][1]) for n in slots]
        if len(done) == 2 and done[0][0] is done[1][0] and sum(done[0][1]) == done[1][1][0]:
            to_sibling(done[0][0], (done[0][1][0], done[0][1][1] + done[1][1][1]))
        else:
            for block, part in done:
                to_sibling(block, part)

    send(here[0], B, zp, 0)
    send(here[0], B, zm, 1)
    send(here[0], A, yn, 2)
    send(here[0], A, zp, 3)
    send(here[0], A, zm, 4)
    send(here[0], B, yn, 17)
    to_sibling(here[0], WHOLE)

    @pl.when(rep == 0)
    def _():
        @pl.loop(1, TPS)
        def _(k):
            pl.semaphore_signal(barrier, inc=1, device_id=(1, lax.rem(tp + k, TPS)), device_id_type=MESH)

    loads[3].wait()
    length = [len_s[s] for s in range(SESSIONS)]
    loads[4].wait()
    for s in range(SESSIONS):
        for t in range(STEPS):
            for q in range(GROUP):
                qrows[s, pl.ds(t * GROUP + q, 1), :] = qbuf[t, pl.ds(s, 1), pl.ds(q * HEAD_DIM, HEAD_DIM)].astype(F32)

    def score(s):
        loads[5 + s].wait()
        q = qrows[s].astype(BF16)

        def body(i, largest):
            start = pl.multiple_of(i * CHUNK, CHUNK)
            part = lax.dot_general(
                q, kbuf[s, pl.ds(start, CHUNK), :], (((1,), (1,)), ((), ())), preferred_element_type=F32) * SCALE
            slot = lax.broadcasted_iota(jnp.int32, (QROWS, CHUNK), 1) + start
            part = jnp.where(slot < length[s], part, -jnp.inf)
            scores[s, :, pl.ds(start, CHUNK)] = part
            for j in range(CHUNK // HEAD_DIM):
                largest = jnp.maximum(largest, part[:, j * HEAD_DIM : (j + 1) * HEAD_DIM])
            return largest

        largest = lax.fori_loop(0, SLOTS // CHUNK, body, jnp.full((QROWS, HEAD_DIM), -jnp.inf, F32))
        return jnp.max(largest, axis=1, keepdims=True)

    def weigh(s, top):
        loads[7 + s].wait()

        def body(i, carry):
            total, acc = carry
            start = pl.multiple_of(i * CHUNK, CHUNK)
            p = jnp.exp(scores[s, :, pl.ds(start, CHUNK)] - top)
            for j in range(CHUNK // HEAD_DIM):
                total = total + p[:, j * HEAD_DIM : (j + 1) * HEAD_DIM]
            acc = acc + jnp.dot(p.astype(BF16), vbuf[s, pl.ds(start, CHUNK), :], preferred_element_type=F32)
            return total, acc

        zero = jnp.zeros((QROWS, HEAD_DIM), F32)
        total, acc = lax.fori_loop(0, SLOTS // CHUNK, body, (zero, zero))
        return jnp.sum(total, axis=1, keepdims=True), acc

    top = [None, None]
    total = [None, None]
    acc = [None, None]
    top[0] = score(0)
    top[1] = score(1)

    pltpu.make_async_copy(hrecv.at[pl.ds(0, REPS - 1)], hrecv.at[pl.ds(0, REPS - 1)], small_recv.at[0]).wait()
    for r in range(REPS):
        for t in range(STEPS):
            hall[pl.ds(r * TOKENS + t * SESSIONS, SESSIONS), :] = hrecv[r, t].astype(F32)
    product = jnp.dot(hall[...].astype(BF16), pooled[rep], preferred_element_type=F32)
    for r in range(REPS):
        psend[r] = product[r * TOKENS : (r + 1) * TOKENS, :].astype(BF16)

    @pl.loop(1, REPS)
    def _(k):
        peer = lax.rem(rep + k, REPS)
        small(psend.at[peer], precv.at[rep], 1, (peer, tp)).start()

    precv[rep] = psend[rep]

    events(0, 1)
    events(2)
    total[0], acc[0] = weigh(0, top[0])
    total[1], acc[1] = weigh(1, top[1])
    events(3, 4)

    @pl.when(tp < TPS // 2)
    def _():
        events(5, 6)

    row = lax.broadcasted_iota(jnp.int32, (TOKENS, HEAD_DIM), 0)
    lane = lax.broadcasted_iota(jnp.int32, (TOKENS, HEAD_DIM), 1)
    position = jnp.where(row % 2 == 0, length[0], length[1]) + row // 2
    angle = position.astype(F32) * frequencies((TOKENS, HEAD_DIM))
    cosine = jnp.cos(angle)
    sine = jnp.where(lane < HEAD_DIM // 2, -jnp.sin(angle), jnp.sin(angle))
    lhs[...] = jnp.zeros(lhs.shape, F32)

    pltpu.make_async_copy(precv.at[pl.ds(0, REPS - 1)], precv.at[pl.ds(0, REPS - 1)], small_recv.at[1]).wait()
    projected = precv[0].astype(F32)
    for r in range(1, REPS):
        projected = projected + precv[r].astype(F32)
    raw = projected[:, :HEAD_DIM]
    swapped = jnp.concatenate([raw[:, HEAD_DIM // 2 :], raw[:, : HEAD_DIM // 2]], axis=1)
    new_keys = (raw * cosine + swapped * sine).astype(BF16)
    new_values = projected[:, HEAD_DIM:].astype(BF16)
    for t in range(STEPS):
        appended[t, :, pl.ds(0, HEAD_DIM)] = new_keys[t * SESSIONS : (t + 1) * SESSIONS, :]
        appended[t, :, pl.ds(HEAD_DIM, HEAD_DIM)] = new_values[t * SESSIONS : (t + 1) * SESSIONS, :]
    new_keys = new_keys.astype(F32)
    new_values = new_values.astype(F32)
    second = lax.broadcasted_iota(jnp.int32, (QROWS, 1), 0) >= GROUP
    for s in range(SESSIONS):
        q = qrows[s]
        fresh = [
            jnp.sum(q * new_keys[u * SESSIONS + s : u * SESSIONS + s + 1, :], axis=1, keepdims=True) * SCALE
            for u in range(STEPS)]
        fresh[1] = jnp.where(second, fresh[1], -jnp.inf)
        peak = jnp.maximum(top[s], jnp.maximum(fresh[0], fresh[1]))
        keep = jnp.exp(top[s] - peak)
        fresh = [jnp.exp(x - peak) for x in fresh]
        whole = total[s] * keep + fresh[0] + fresh[1]
        out = acc[s] * (keep / whole)
        for u in range(STEPS):
            out = out + (fresh[u] / whole).astype(BF16).astype(F32) * new_values[u * SESSIONS + s : u * SESSIONS + s + 1, :]
        heads[s] = out
    for s in range(SESSIONS):
        for t in range(STEPS):
            for q in range(GROUP):
                lhs[pl.ds(t * SESSIONS + s, 1), pl.ds(q * HEAD_DIM, HEAD_DIM)] = heads[s, pl.ds(t * GROUP + q, 1), :]
    left = lhs[...].astype(BF16)
    loads[9].wait()

    @pl.when(rep != 1)
    def _():
        pl.semaphore_wait(ready, 1)

    @pl.when(rep == 1)
    def _():
        pl.semaphore_wait(barrier, TPS - 1)

        @pl.loop(0, REPS)
        def _(k):
            @pl.when(k != 1)
            def _():
                pl.semaphore_signal(ready, inc=1, device_id=(k, tp), device_id_type=MESH)

    for part in range(PARTS):
        @pl.loop(0, PART // OUT_COLS)
        def _(i):
            start = pl.multiple_of(i * OUT_COLS, OUT_COLS)
            result = jnp.dot(left, wbuf[:, pl.ds(part * PART + start, OUT_COLS)], preferred_element_type=F32)
            osend[part, :, pl.ds(start, OUT_COLS)] = result[:TOKENS].astype(BF16)

        @pl.loop(1, TPS)
        def _(k):
            small(osend.at[part], orecv.at[part, tp], 2, (rep, lax.rem(tp + k, TPS))).start()

    @pl.when(tp >= TPS // 2)
    def _():
        events(5, 6)

    events(11, 12)
    events(17)
    events(7, 8)
    events(13, 14)
    events(9, 10)
    events(15, 16)

    def drain(ref, sem):
        pltpu.make_async_copy(ref, ref, sem).wait()

    arrived(there[2], A0_END, 18)
    arrived(far_other, A0_END, 19)
    arrived(there[2], A1_END, 20)
    arrived(far_other, A1_END, 21)
    others = orecv.at[:, pl.ds(0, TPS - 1)]
    drain(others, small_recv.at[2])
    for part in range(PARTS):
        orecv[part, tp] = osend[part]
        for i in range(PART // OUT_COLS):
            columns = pl.ds(i * OUT_COLS, OUT_COLS)
            summed = orecv[part, 0, :, columns].astype(F32)
            for r in range(1, TPS):
                summed = summed + orecv[part, r, :, columns].astype(F32)
            summed = summed.astype(BF16)
            for t in range(STEPS):
                attended[t, :, pl.ds(part * PART + i * OUT_COLS, OUT_COLS)] = summed[t * SESSIONS : (t + 1) * SESSIONS, :]
    drain(pooled.at[pl.ds(0, REPS // 2), pl.ds(0, ROWS - 16)], sib_recv)
    drain(pooled.at[pl.ds(0, REPS - 1)], bulk_send)
    drain(hsend.at[pl.ds(0, REPS - 1)], small_send.at[0])
    drain(psend.at[pl.ds(0, REPS - 1)], small_send.at[1])
    drain(others, small_send.at[2])


def write_kernel(owners, pooled, attended, appended, installed, attended_out, appended_out, sem):
    copies = [
        pltpu.make_async_copy(pooled.at[owners[s]], installed.at[s], sem.at[s]) for s in range(REPS)]
    copies.append(pltpu.make_async_copy(attended, attended_out, sem.at[REPS]))
    copies.append(pltpu.make_async_copy(appended, appended_out, sem.at[REPS + 1]))
    for copy in copies:
        copy.start()
    for copy in copies:
        copy.wait()


def shards(hidden, queries, sectioned, owners, keys, values, lengths, weight):
    operands = [
        pltpu.with_memory_space_constraint(x, pltpu.HBM)
        for x in (hidden, queries, sectioned, owners, keys, values, lengths, weight)]
    hbm = pl.BlockSpec(memory_space=pltpu.HBM)
    vmem = pl.BlockSpec(memory_space=pltpu.VMEM)
    pooled, attended, appended = pl.pallas_call(
        main_kernel,
        out_shape=(
            pltpu.VMEM((REPS, ROWS, COLS), BF16),
            pltpu.VMEM((STEPS, SESSIONS, PARTS * PART), BF16),
            pltpu.VMEM((STEPS, SESSIONS, COLS), BF16),
        ),
        in_specs=[hbm] * 8,
        out_specs=(vmem, vmem, vmem),
        scratch_shapes=[
            pltpu.VMEM((SESSIONS, SLOTS, HEAD_DIM), BF16),
            pltpu.VMEM((SESSIONS, SLOTS, HEAD_DIM), BF16),
            pltpu.VMEM((GROUP * HEAD_DIM, PARTS * PART), BF16),
            pltpu.VMEM((STEPS, SESSIONS, REPS * ROWS), BF16),
            pltpu.VMEM((STEPS, SESSIONS, GROUP * HEAD_DIM), BF16),
            pltpu.SMEM((REPS,), jnp.int32),
            pltpu.SMEM((SESSIONS,), jnp.int32),
            pltpu.VMEM((REPS, STEPS, SESSIONS, ROWS), BF16),
            pltpu.VMEM((REPS, STEPS, SESSIONS, ROWS), BF16),
            pltpu.VMEM((REPS, STEPS, SESSIONS, ROWS), BF16),
            pltpu.VMEM((REPS * TOKENS, ROWS), F32),
            pltpu.VMEM((REPS, TOKENS, COLS), BF16),
            pltpu.VMEM((REPS, TOKENS, COLS), BF16),
            pltpu.VMEM((SESSIONS, QROWS, HEAD_DIM), F32),
            pltpu.VMEM((SESSIONS, QROWS, SLOTS), F32),
            pltpu.VMEM((SESSIONS, QROWS, HEAD_DIM), F32),
            pltpu.VMEM((8, GROUP * HEAD_DIM), F32),
            pltpu.VMEM((PARTS, TOKENS, PART), BF16),
            pltpu.VMEM((PARTS, TPS, TOKENS, PART), BF16),
            pltpu.SemaphoreType.DMA((10,)),
            pltpu.SemaphoreType.DMA,
            pltpu.SemaphoreType.DMA((22,)),
            pltpu.SemaphoreType.DMA,
            pltpu.SemaphoreType.DMA((3,)),
            pltpu.SemaphoreType.DMA((3,)),
            pltpu.SemaphoreType.REGULAR,
        ],
        compiler_params=pltpu.CompilerParams(
            collective_id=0, has_side_effects=True, vmem_limit_bytes=32 << 20),
        name="gather_and_attend",
    )(*operands)
    installed, attended, appended = pl.pallas_call(
        write_kernel,
        out_shape=(
            jax.ShapeDtypeStruct((REPS, ROWS, COLS), BF16),
            jax.ShapeDtypeStruct(attended.shape, BF16),
            jax.ShapeDtypeStruct(appended.shape, BF16),
        ),
        grid_spec=pltpu.PrefetchScalarGridSpec(
            num_scalar_prefetch=1,
            grid=(),
            in_specs=[vmem, vmem, vmem],
            out_specs=(hbm, hbm, hbm),
            scratch_shapes=[pltpu.SemaphoreType.DMA((REPS + 2,))],
        ),
        compiler_params=pltpu.CompilerParams(vmem_limit_bytes=4 << 20),
        name="write_in_order",
    )(owners, pooled, attended, appended)
    return installed.reshape(REPS * ROWS, COLS), appended, attended


def solution(mesh):
    in_specs = (
        P(None, "rep", None),
        P(None, "rep", "tp"),
        P("rep", "tp"),
        P(),
        P("rep", None, "tp"),
        P("rep", None, "tp"),
        P("rep"),
        P("tp", None),
    )
    out_specs = (P(None, "tp"), P(None, "rep", "tp"), P(None, "rep", None))
    return jax.shard_map(shards, mesh=mesh, in_specs=in_specs, out_specs=out_specs, check_vma=False)
```

```python
import functools
import math

import jax
import jax.numpy as jnp
from jax import lax
from jax.experimental import pallas as pl
from jax.experimental.pallas import tpu as pltpu
from jax.sharding import PartitionSpec as P

HEAD_DIM = 128
ROPE_BASE = 500000.0
SCALE = HEAD_DIM**-0.5
MESH = pl.DeviceIdType.MESH
F32 = jnp.float32
BF16 = jnp.bfloat16

REPS = 16
HERALD = 2
COLLECTOR = 3
TPS = 8
ROWS = 512
COLS = 256
STEPS = 2
SESSIONS = 2
TOKENS = STEPS * SESSIONS
GROUP = 8
QROWS = STEPS * GROUP
SLOTS = 8192
CHUNK = 2048
OUT_COLS = 512
PARTS = 4
PART = 1024

A0 = (0, 160)
A1 = (160, 176)
A = (0, 336)
B0 = (336, 80)
B1 = (416, 96)
B = (336, 176)
A0_MOST, A0_END = (0, 96), (96, 64)
A1_MOST, A1_END = (160, 112), (272, 64)
WHOLE = (0, 512)


def frequencies(shape):
    lane = lax.broadcasted_iota(jnp.int32, shape, 1) % (HEAD_DIM // 2)
    result = jnp.ones(shape, F32)
    for bit in range(6):
        factor = math.exp(-math.log(ROPE_BASE) * (1 << bit) / (HEAD_DIM // 2))
        result = result * jnp.where((lane // (1 << bit)) % 2 == 1, factor, 1.0).astype(F32)
    return result


def main_kernel(
    hidden, queries, sectioned, owners, keys, values, lengths, weight,
    pooled, attended, appended,
    kbuf, vbuf, wbuf, hbuf, qbuf, own_s, len_s, hsplit, hsend, hrecv, hall, psend, precv,
    qrows, scores, heads, lhs, osend, orecv,
    load_sem, bulk_send, bulk_recv, sib_recv, small_send, small_recv, ready,
):
    rep = lax.axis_index("rep")
    tp = lax.axis_index("tp")
    y, z, c = rep // 8, (rep // 2) % 4, rep % 2

    def chip(yy, zz, cc):
        return yy * 8 + lax.rem(zz + 4, 4) * 2 + cc

    zp = (chip(y, z + 1, c), tp)
    zm = (chip(y, z - 1, c), tp)
    yn = (chip(1 - y, z, c), tp)
    sib = (chip(y, z, 1 - c), tp)
    zp_other = (chip(y, z + 1, 1 - c), tp)
    zm_other = (chip(y, z - 1, 1 - c), tp)
    far_other = chip(1 - y, z + 2, 1 - c)

    loads = [
        pltpu.make_async_copy(owners, own_s, load_sem.at[0]),
        pltpu.make_async_copy(hidden, hbuf, load_sem.at[1]),
        pltpu.make_async_copy(sectioned, pooled.at[rep], load_sem.at[2]),
        pltpu.make_async_copy(lengths, len_s, load_sem.at[3]),
        pltpu.make_async_copy(queries, qbuf, load_sem.at[4]),
        pltpu.make_async_copy(keys.at[0], kbuf.at[0], load_sem.at[5]),
        pltpu.make_async_copy(keys.at[1], kbuf.at[1], load_sem.at[6]),
        pltpu.make_async_copy(values.at[0], vbuf.at[0], load_sem.at[7]),
        pltpu.make_async_copy(values.at[1], vbuf.at[1], load_sem.at[8]),
        pltpu.make_async_copy(weight, wbuf, load_sem.at[9]),
    ]
    for load in loads[:5]:
        load.start()

    barrier = pltpu.get_barrier_semaphore()

    @pl.loop(0, REPS)
    def _(k):
        @pl.when((k != rep) & (k != COLLECTOR))
        def _():
            pl.semaphore_signal(barrier, inc=1, device_id=(k, tp), device_id_type=MESH)

    loads[1].wait()
    for r in range(REPS):
        for t in range(STEPS):
            hsplit[r, t] = hbuf[t, :, pl.ds(r * ROWS, ROWS)]
    loads[0].wait()
    owner = [own_s[s] for s in range(REPS)]
    for r in range(REPS):
        found = jnp.int32(0)
        for s in range(1, REPS):
            found = jnp.where(owner[s] == r, s, found)
        hsend[r] = hsplit[found]

    loads[2].wait()
    for load in loads[5:]:
        load.start()

    @pl.when(rep != COLLECTOR)
    def _():
        pl.semaphore_wait(barrier, REPS - 1)

    @pl.when(rep == HERALD)
    def _():
        pl.semaphore_signal(ready, inc=1, device_id=(COLLECTOR, tp), device_id_type=MESH)

    @pl.when(rep == COLLECTOR)
    def _():
        pl.semaphore_wait(ready, 1)

    def small(src, dst, which, device):
        return pltpu.make_async_remote_copy(
            src_ref=src, dst_ref=dst, send_sem=small_send.at[which], recv_sem=small_recv.at[which],
            device_id=device, device_id_type=MESH)

    @pl.loop(1, REPS)
    def _(k):
        peer = lax.rem(rep + k, REPS)
        small(hsend.at[peer], hrecv.at[rep], 0, (peer, tp)).start()

    hrecv[rep] = hsend[rep]

    def piece(block, part):
        return pooled.at[block, pl.ds(*part), :]

    def send(block, part, device, slot):
        ref = piece(block, part)
        pltpu.make_async_remote_copy(
            src_ref=ref, dst_ref=ref, send_sem=bulk_send, recv_sem=bulk_recv.at[slot],
            device_id=device, device_id_type=MESH).start()

    def to_sibling(block, part):
        ref = piece(block, part)
        pltpu.make_async_remote_copy(
            src_ref=ref, dst_ref=ref, send_sem=bulk_send, recv_sem=sib_recv,
            device_id=sib, device_id_type=MESH).start()

    def arrived(block, part, slot):
        ref = piece(block, part)
        pltpu.make_async_copy(ref, ref, bulk_recv.at[slot]).wait()

    here = {
        0: chip(y, z, c), 1: chip(y, z + 1, c), -1: chip(y, z - 1, c), 2: chip(y, z + 2, c)}
    there = {
        0: chip(1 - y, z, c), 1: chip(1 - y, z + 1, c), -1: chip(1 - y, z - 1, c), 2: chip(1 - y, z + 2, c)}

    route = [
        (here[-1], B, [(zp, B0, 5), (yn, B, 7)]),
        (here[1], B, [(zm, B1, 6), (yn, B, 8)]),
        (there[0], A, [(zp, A, 11), (zm, A, 12)]),
        (here[-1], A, [(zp, A0, 13)]),
        (here[1], A, [(zm, A1, 14)]),
        (here[2], B0, [(yn, B0, 9)]),
        (here[2], B1, [(yn, B1, 10)]),
        (there[-1], B, []),
        (there[1], B, []),
        (there[2], B0, []),
        (there[2], B1, []),
        (there[-1], A, [(zp, A0_MOST, 15), (zp, A0_END, 18), (zp_other, A0_END, 19)]),
        (there[1], A, [(zm, A1_MOST, 16), (zm, A1_END, 20), (zm_other, A1_END, 21)]),
        (here[2], A0, []),
        (here[2], A1, []),
        (there[2], A0_MOST, []),
        (there[2], A1_MOST, []),
        (there[0], B, []),
    ]

    def events(*slots):
        for n in slots:
            block, part, onward = route[n]
            arrived(block, part, n)
            for device, onward_part, slot in onward:
                send(block, onward_part, device, slot)
        done = [(route[n][0], route[n][1]) for n in slots]
        if len(done) == 2 and done[0][0] is done[1][0] and sum(done[0][1]) == done[1][1][0]:
            to_sibling(done[0][0], (done[0][1][0], done[0][1][1] + done[1][1][1]))
        else:
            for block, part in done:
                to_sibling(block, part)

    send(here[0], B, zp, 0)
    send(here[0], B, zm, 1)
    send(here[0], A, yn, 2)
    send(here[0], A, zp, 3)
    send(here[0], A, zm, 4)
    send(here[0], B, yn, 17)
    to_sibling(here[0], WHOLE)

    @pl.when(rep == HERALD)
    def _():
        @pl.loop(1, TPS)
        def _(k):
            pl.semaphore_signal(barrier, inc=1, device_id=(COLLECTOR, lax.rem(tp + k, TPS)), device_id_type=MESH)

    loads[3].wait()
    length = [len_s[s] for s in range(SESSIONS)]
    loads[4].wait()
    for s in range(SESSIONS):
        for t in range(STEPS):
            for q in range(GROUP):
                qrows[s, pl.ds(t * GROUP + q, 1), :] = qbuf[t, pl.ds(s, 1), pl.ds(q * HEAD_DIM, HEAD_DIM)].astype(F32)

    def score(s):
        loads[5 + s].wait()
        q = qrows[s].astype(BF16)

        def body(i, largest):
            start = pl.multiple_of(i * CHUNK, CHUNK)
            part = lax.dot_general(
                q, kbuf[s, pl.ds(start, CHUNK), :], (((1,), (1,)), ((), ())), preferred_element_type=F32) * SCALE
            slot = lax.broadcasted_iota(jnp.int32, (QROWS, CHUNK), 1) + start
            part = jnp.where(slot < length[s], part, -jnp.inf)
            scores[s, :, pl.ds(start, CHUNK)] = part
            for j in range(CHUNK // HEAD_DIM):
                largest = jnp.maximum(largest, part[:, j * HEAD_DIM : (j + 1) * HEAD_DIM])
            return largest

        largest = lax.fori_loop(0, SLOTS // CHUNK, body, jnp.full((QROWS, HEAD_DIM), -jnp.inf, F32))
        return jnp.max(largest, axis=1, keepdims=True)

    def weigh(s, top):
        loads[7 + s].wait()

        def body(i, carry):
            total, acc = carry
            start = pl.multiple_of(i * CHUNK, CHUNK)
            p = jnp.exp(scores[s, :, pl.ds(start, CHUNK)] - top)
            for j in range(CHUNK // HEAD_DIM):
                total = total + p[:, j * HEAD_DIM : (j + 1) * HEAD_DIM]
            acc = acc + jnp.dot(p.astype(BF16), vbuf[s, pl.ds(start, CHUNK), :], preferred_element_type=F32)
            return total, acc

        zero = jnp.zeros((QROWS, HEAD_DIM), F32)
        total, acc = lax.fori_loop(0, SLOTS // CHUNK, body, (zero, zero))
        return jnp.sum(total, axis=1, keepdims=True), acc

    top = [None, None]
    total = [None, None]
    acc = [None, None]
    top[0] = score(0)
    top[1] = score(1)

    pltpu.make_async_copy(hrecv.at[pl.ds(0, REPS - 1)], hrecv.at[pl.ds(0, REPS - 1)], small_recv.at[0]).wait()
    for r in range(REPS):
        for t in range(STEPS):
            hall[pl.ds(r * TOKENS + t * SESSIONS, SESSIONS), :] = hrecv[r, t].astype(F32)
    product = jnp.dot(hall[...].astype(BF16), pooled[rep], preferred_element_type=F32)
    for r in range(REPS):
        psend[r] = product[r * TOKENS : (r + 1) * TOKENS, :].astype(BF16)

    @pl.loop(1, REPS)
    def _(k):
        peer = lax.rem(rep + k, REPS)
        small(psend.at[peer], precv.at[rep], 1, (peer, tp)).start()

    precv[rep] = psend[rep]

    events(0, 1)
    events(2)
    total[0], acc[0] = weigh(0, top[0])
    total[1], acc[1] = weigh(1, top[1])
    events(3, 4)


    row = lax.broadcasted_iota(jnp.int32, (TOKENS, HEAD_DIM), 0)
    lane = lax.broadcasted_iota(jnp.int32, (TOKENS, HEAD_DIM), 1)
    position = jnp.where(row % 2 == 0, length[0], length[1]) + row // 2
    angle = position.astype(F32) * frequencies((TOKENS, HEAD_DIM))
    cosine = jnp.cos(angle)
    sine = jnp.where(lane < HEAD_DIM // 2, -jnp.sin(angle), jnp.sin(angle))
    lhs[...] = jnp.zeros(lhs.shape, F32)

    @pl.when(rep == COLLECTOR)
    def _():
        pl.semaphore_wait(barrier, TPS - 1)

        @pl.loop(0, REPS)
        def _(k):
            @pl.when(k != COLLECTOR)
            def _():
                pl.semaphore_signal(ready, inc=1, device_id=(k, tp), device_id_type=MESH)

    pltpu.make_async_copy(precv.at[pl.ds(0, REPS - 1)], precv.at[pl.ds(0, REPS - 1)], small_recv.at[1]).wait()
    projected = precv[0].astype(F32)
    for r in range(1, REPS):
        projected = projected + precv[r].astype(F32)
    raw = projected[:, :HEAD_DIM]
    swapped = jnp.concatenate([raw[:, HEAD_DIM // 2 :], raw[:, : HEAD_DIM // 2]], axis=1)
    new_keys = (raw * cosine + swapped * sine).astype(BF16)
    new_values = projected[:, HEAD_DIM:].astype(BF16)
    for t in range(STEPS):
        appended[t, :, pl.ds(0, HEAD_DIM)] = new_keys[t * SESSIONS : (t + 1) * SESSIONS, :]
        appended[t, :, pl.ds(HEAD_DIM, HEAD_DIM)] = new_values[t * SESSIONS : (t + 1) * SESSIONS, :]
    new_keys = new_keys.astype(F32)
    new_values = new_values.astype(F32)
    second = lax.broadcasted_iota(jnp.int32, (QROWS, 1), 0) >= GROUP
    for s in range(SESSIONS):
        q = qrows[s]
        fresh = [
            jnp.sum(q * new_keys[u * SESSIONS + s : u * SESSIONS + s + 1, :], axis=1, keepdims=True) * SCALE
            for u in range(STEPS)]
        fresh[1] = jnp.where(second, fresh[1], -jnp.inf)
        peak = jnp.maximum(top[s], jnp.maximum(fresh[0], fresh[1]))
        keep = jnp.exp(top[s] - peak)
        fresh = [jnp.exp(x - peak) for x in fresh]
        whole = total[s] * keep + fresh[0] + fresh[1]
        out = acc[s] * (keep / whole)
        for u in range(STEPS):
            out = out + (fresh[u] / whole).astype(BF16).astype(F32) * new_values[u * SESSIONS + s : u * SESSIONS + s + 1, :]
        heads[s] = out
    for s in range(SESSIONS):
        for t in range(STEPS):
            for q in range(GROUP):
                lhs[pl.ds(t * SESSIONS + s, 1), pl.ds(q * HEAD_DIM, HEAD_DIM)] = heads[s, pl.ds(t * GROUP + q, 1), :]
    events(5, 6)
    left = lhs[...].astype(BF16)
    loads[9].wait()

    @pl.when(rep != COLLECTOR)
    def _():
        pl.semaphore_wait(ready, 1)

    for part in range(PARTS):
        @pl.loop(0, PART // OUT_COLS)
        def _(i):
            start = pl.multiple_of(i * OUT_COLS, OUT_COLS)
            result = jnp.dot(left, wbuf[:, pl.ds(part * PART + start, OUT_COLS)], preferred_element_type=F32)
            osend[part, :, pl.ds(start, OUT_COLS)] = result[:TOKENS].astype(BF16)

        @pl.loop(1, TPS)
        def _(k):
            small(osend.at[part], orecv.at[part, tp], 2, (rep, lax.rem(tp + k, TPS))).start()

    events(11, 12)
    events(17)
    events(7, 8)
    events(13, 14)
    events(9, 10)
    events(15, 16)

    def drain(ref, sem):
        pltpu.make_async_copy(ref, ref, sem).wait()

    arrived(there[2], A0_END, 18)
    arrived(far_other, A0_END, 19)
    arrived(there[2], A1_END, 20)
    arrived(far_other, A1_END, 21)
    others = orecv.at[:, pl.ds(0, TPS - 1)]
    drain(others, small_recv.at[2])
    for part in range(PARTS):
        orecv[part, tp] = osend[part]
        for i in range(PART // OUT_COLS):
            columns = pl.ds(i * OUT_COLS, OUT_COLS)
            summed = orecv[part, 0, :, columns].astype(F32)
            for r in range(1, TPS):
                summed = summed + orecv[part, r, :, columns].astype(F32)
            summed = summed.astype(BF16)
            for t in range(STEPS):
                attended[t, :, pl.ds(part * PART + i * OUT_COLS, OUT_COLS)] = summed[t * SESSIONS : (t + 1) * SESSIONS, :]
    drain(pooled.at[pl.ds(0, REPS // 2), pl.ds(0, ROWS - 16)], sib_recv)
    drain(pooled.at[pl.ds(0, REPS - 1)], bulk_send)
    drain(hsend.at[pl.ds(0, REPS - 1)], small_send.at[0])
    drain(psend.at[pl.ds(0, REPS - 1)], small_send.at[1])
    drain(others, small_send.at[2])


def write_kernel(owners, pooled, attended, appended, installed, attended_out, appended_out, sem):
    copies = [
        pltpu.make_async_copy(pooled.at[owners[s]], installed.at[s], sem.at[s]) for s in range(REPS)]
    copies.append(pltpu.make_async_copy(attended, attended_out, sem.at[REPS]))
    copies.append(pltpu.make_async_copy(appended, appended_out, sem.at[REPS + 1]))
    for copy in copies:
        copy.start()
    for copy in copies:
        copy.wait()


def shards(hidden, queries, sectioned, owners, keys, values, lengths, weight):
    operands = [
        pltpu.with_memory_space_constraint(x, pltpu.HBM)
        for x in (hidden, queries, sectioned, owners, keys, values, lengths, weight)]
    hbm = pl.BlockSpec(memory_space=pltpu.HBM)
    vmem = pl.BlockSpec(memory_space=pltpu.VMEM)
    pooled, attended, appended = pl.pallas_call(
        main_kernel,
        out_shape=(
            pltpu.VMEM((REPS, ROWS, COLS), BF16),
            pltpu.VMEM((STEPS, SESSIONS, PARTS * PART), BF16),
            pltpu.VMEM((STEPS, SESSIONS, COLS), BF16),
        ),
        in_specs=[hbm] * 8,
        out_specs=(vmem, vmem, vmem),
        scratch_shapes=[
            pltpu.VMEM((SESSIONS, SLOTS, HEAD_DIM), BF16),
            pltpu.VMEM((SESSIONS, SLOTS, HEAD_DIM), BF16),
            pltpu.VMEM((GROUP * HEAD_DIM, PARTS * PART), BF16),
            pltpu.VMEM((STEPS, SESSIONS, REPS * ROWS), BF16),
            pltpu.VMEM((STEPS, SESSIONS, GROUP * HEAD_DIM), BF16),
            pltpu.SMEM((REPS,), jnp.int32),
            pltpu.SMEM((SESSIONS,), jnp.int32),
            pltpu.VMEM((REPS, STEPS, SESSIONS, ROWS), BF16),
            pltpu.VMEM((REPS, STEPS, SESSIONS, ROWS), BF16),
            pltpu.VMEM((REPS, STEPS, SESSIONS, ROWS), BF16),
            pltpu.VMEM((REPS * TOKENS, ROWS), F32),
            pltpu.VMEM((REPS, TOKENS, COLS), BF16),
            pltpu.VMEM((REPS, TOKENS, COLS), BF16),
            pltpu.VMEM((SESSIONS, QROWS, HEAD_DIM), F32),
            pltpu.VMEM((SESSIONS, QROWS, SLOTS), F32),
            pltpu.VMEM((SESSIONS, QROWS, HEAD_DIM), F32),
            pltpu.VMEM((8, GROUP * HEAD_DIM), F32),
            pltpu.VMEM((PARTS, TOKENS, PART), BF16),
            pltpu.VMEM((PARTS, TPS, TOKENS, PART), BF16),
            pltpu.SemaphoreType.DMA((10,)),
            pltpu.SemaphoreType.DMA,
            pltpu.SemaphoreType.DMA((22,)),
            pltpu.SemaphoreType.DMA,
            pltpu.SemaphoreType.DMA((3,)),
            pltpu.SemaphoreType.DMA((3,)),
            pltpu.SemaphoreType.REGULAR,
        ],
        compiler_params=pltpu.CompilerParams(
            collective_id=0, has_side_effects=True, vmem_limit_bytes=32 << 20),
        name="gather_and_attend",
    )(*operands)
    installed, attended, appended = pl.pallas_call(
        write_kernel,
        out_shape=(
            jax.ShapeDtypeStruct((REPS, ROWS, COLS), BF16),
            jax.ShapeDtypeStruct(attended.shape, BF16),
            jax.ShapeDtypeStruct(appended.shape, BF16),
        ),
        grid_spec=pltpu.PrefetchScalarGridSpec(
            num_scalar_prefetch=1,
            grid=(),
            in_specs=[vmem, vmem, vmem],
            out_specs=(hbm, hbm, hbm),
            scratch_shapes=[pltpu.SemaphoreType.DMA((REPS + 2,))],
        ),
        compiler_params=pltpu.CompilerParams(vmem_limit_bytes=4 << 20),
        name="write_in_order",
    )(owners, pooled, attended, appended)
    return installed.reshape(REPS * ROWS, COLS), appended, attended


def solution(mesh):
    in_specs = (
        P(None, "rep", None),
        P(None, "rep", "tp"),
        P("rep", "tp"),
        P(),
        P("rep", None, "tp"),
        P("rep", None, "tp"),
        P("rep"),
        P("tp", None),
    )
    out_specs = (P(None, "tp"), P(None, "rep", "tp"), P(None, "rep", None))
    return jax.shard_map(shards, mesh=mesh, in_specs=in_specs, out_specs=out_specs, check_vma=False)
```

```python
import functools
import math

import jax
import jax.numpy as jnp
from jax import lax
from jax.experimental import pallas as pl
from jax.experimental.pallas import tpu as pltpu
from jax.sharding import PartitionSpec as P

HEAD_DIM = 128
ROPE_BASE = 500000.0
SCALE = HEAD_DIM**-0.5
MESH = pl.DeviceIdType.MESH
F32 = jnp.float32
BF16 = jnp.bfloat16

REPS = 16
HERALD = 2
COLLECTOR = 3
TPS = 8
ROWS = 512
COLS = 256
STEPS = 2
SESSIONS = 2
TOKENS = STEPS * SESSIONS
GROUP = 8
QROWS = STEPS * GROUP
SLOTS = 8192
CHUNK = 2048
OUT_COLS = 512
PARTS = 4
PART = 1024

A0 = (0, 160)
A1 = (160, 176)
A = (0, 336)
B0 = (336, 80)
B1 = (416, 96)
B = (336, 176)
A0_MOST, A0_END = (0, 96), (96, 64)
A1_MOST, A1_END = (160, 112), (272, 64)
WHOLE = (0, 512)


def frequencies(shape):
    lane = lax.broadcasted_iota(jnp.int32, shape, 1) % (HEAD_DIM // 2)
    result = jnp.ones(shape, F32)
    for bit in range(6):
        factor = math.exp(-math.log(ROPE_BASE) * (1 << bit) / (HEAD_DIM // 2))
        result = result * jnp.where((lane // (1 << bit)) % 2 == 1, factor, 1.0).astype(F32)
    return result


def main_kernel(
    hidden, queries, sectioned, owners, keys, values, lengths, weight,
    pooled, attended, appended,
    kbuf, vbuf, wbuf, hbuf, qbuf, own_s, len_s, hsplit, hsend, hrecv, hall, psend, precv,
    qrows, scores, heads, lhs, osend, orecv,
    load_sem, bulk_send, bulk_recv, sib_recv, small_send, small_recv, ready,
):
    rep = lax.axis_index("rep")
    tp = lax.axis_index("tp")
    y, z, c = rep // 8, (rep // 2) % 4, rep % 2

    def chip(yy, zz, cc):
        return yy * 8 + lax.rem(zz + 4, 4) * 2 + cc

    zp = (chip(y, z + 1, c), tp)
    zm = (chip(y, z - 1, c), tp)
    yn = (chip(1 - y, z, c), tp)
    sib = (chip(y, z, 1 - c), tp)
    zp_other = (chip(y, z + 1, 1 - c), tp)
    zm_other = (chip(y, z - 1, 1 - c), tp)
    far_other = chip(1 - y, z + 2, 1 - c)

    barrier = pltpu.get_barrier_semaphore()

    @pl.loop(0, REPS)
    def _(k):
        @pl.when((k != rep) & (k != COLLECTOR))
        def _():
            pl.semaphore_signal(barrier, inc=1, device_id=(k, tp), device_id_type=MESH)

    loads = [
        pltpu.make_async_copy(owners, own_s, load_sem.at[0]),
        pltpu.make_async_copy(hidden, hbuf, load_sem.at[1]),
        pltpu.make_async_copy(sectioned, pooled.at[rep], load_sem.at[2]),
        pltpu.make_async_copy(lengths, len_s, load_sem.at[3]),
        pltpu.make_async_copy(queries, qbuf, load_sem.at[4]),
        pltpu.make_async_copy(keys.at[0], kbuf.at[0], load_sem.at[5]),
        pltpu.make_async_copy(keys.at[1], kbuf.at[1], load_sem.at[6]),
        pltpu.make_async_copy(values.at[0], vbuf.at[0], load_sem.at[7]),
        pltpu.make_async_copy(values.at[1], vbuf.at[1], load_sem.at[8]),
        pltpu.make_async_copy(weight, wbuf, load_sem.at[9]),
    ]
    for load in loads[:5]:
        load.start()

    loads[1].wait()
    for r in range(REPS):
        for t in range(STEPS):
            hsplit[r, t] = hbuf[t, :, pl.ds(r * ROWS, ROWS)]
    loads[0].wait()
    owner = [own_s[s] for s in range(REPS)]
    for r in range(REPS):
        found = jnp.int32(0)
        for s in range(1, REPS):
            found = jnp.where(owner[s] == r, s, found)
        hsend[r] = hsplit[found]

    loads[2].wait()
    for load in loads[5:]:
        load.start()

    @pl.when(rep != COLLECTOR)
    def _():
        pl.semaphore_wait(barrier, REPS - 1)

    @pl.when(rep == HERALD)
    def _():
        pl.semaphore_signal(ready, inc=1, device_id=(COLLECTOR, tp), device_id_type=MESH)

    @pl.when(rep == COLLECTOR)
    def _():
        pl.semaphore_wait(ready, 1)

    def small(src, dst, which, device):
        return pltpu.make_async_remote_copy(
            src_ref=src, dst_ref=dst, send_sem=small_send.at[which], recv_sem=small_recv.at[which],
            device_id=device, device_id_type=MESH)

    @pl.loop(1, REPS)
    def _(k):
        peer = lax.rem(rep + k, REPS)
        small(hsend.at[peer], hrecv.at[rep], 0, (peer, tp)).start()

    hrecv[rep] = hsend[rep]

    def piece(block, part):
        return pooled.at[block, pl.ds(*part), :]

    def send(block, part, device, slot):
        ref = piece(block, part)
        pltpu.make_async_remote_copy(
            src_ref=ref, dst_ref=ref, send_sem=bulk_send, recv_sem=bulk_recv.at[slot],
            device_id=device, device_id_type=MESH).start()

    def to_sibling(block, part):
        ref = piece(block, part)
        pltpu.make_async_remote_copy(
            src_ref=ref, dst_ref=ref, send_sem=bulk_send, recv_sem=sib_recv,
            device_id=sib, device_id_type=MESH).start()

    def arrived(block, part, slot):
        ref = piece(block, part)
        pltpu.make_async_copy(ref, ref, bulk_recv.at[slot]).wait()

    here = {
        0: chip(y, z, c), 1: chip(y, z + 1, c), -1: chip(y, z - 1, c), 2: chip(y, z + 2, c)}
    there = {
        0: chip(1 - y, z, c), 1: chip(1 - y, z + 1, c), -1: chip(1 - y, z - 1, c), 2: chip(1 - y, z + 2, c)}

    route = [
        (here[-1], B, [(zp, B0, 5), (yn, B, 7)]),
        (here[1], B, [(zm, B1, 6), (yn, B, 8)]),
        (there[0], A, [(zp, A, 11), (zm, A, 12)]),
        (here[-1], A, [(zp, A0, 13)]),
        (here[1], A, [(zm, A1, 14)]),
        (here[2], B0, [(yn, B0, 9)]),
        (here[2], B1, [(yn, B1, 10)]),
        (there[-1], B, []),
        (there[1], B, []),
        (there[2], B0, []),
        (there[2], B1, []),
        (there[-1], A, [(zp, A0_MOST, 15), (zp, A0_END, 18), (zp_other, A0_END, 19)]),
        (there[1], A, [(zm, A1_MOST, 16), (zm, A1_END, 20), (zm_other, A1_END, 21)]),
        (here[2], A0, []),
        (here[2], A1, []),
        (there[2], A0_MOST, []),
        (there[2], A1_MOST, []),
        (there[0], B, []),
    ]

    def events(*slots):
        for n in slots:
            block, part, onward = route[n]
            arrived(block, part, n)
            for device, onward_part, slot in onward:
                send(block, onward_part, device, slot)
        done = [(route[n][0], route[n][1]) for n in slots]
        if len(done) == 2 and done[0][0] is done[1][0] and sum(done[0][1]) == done[1][1][0]:
            to_sibling(done[0][0], (done[0][1][0], done[0][1][1] + done[1][1][1]))
        else:
            for block, part in done:
                to_sibling(block, part)

    send(here[0], B, zp, 0)
    send(here[0], B, zm, 1)
    send(here[0], A, yn, 2)
    send(here[0], A, zp, 3)
    send(here[0], A, zm, 4)
    send(here[0], B, yn, 17)
    to_sibling(here[0], WHOLE)

    @pl.when(rep == HERALD)
    def _():
        @pl.loop(1, TPS)
        def _(k):
            pl.semaphore_signal(barrier, inc=1, device_id=(COLLECTOR, lax.rem(tp + k, TPS)), device_id_type=MESH)

    loads[3].wait()
    length = [len_s[s] for s in range(SESSIONS)]
    loads[4].wait()
    for s in range(SESSIONS):
        for t in range(STEPS):
            for q in range(GROUP):
                qrows[s, pl.ds(t * GROUP + q, 1), :] = qbuf[t, pl.ds(s, 1), pl.ds(q * HEAD_DIM, HEAD_DIM)].astype(F32)

    def score(s):
        loads[5 + s].wait()
        q = qrows[s].astype(BF16)

        def body(i, largest):
            start = pl.multiple_of(i * CHUNK, CHUNK)
            part = lax.dot_general(
                q, kbuf[s, pl.ds(start, CHUNK), :], (((1,), (1,)), ((), ())), preferred_element_type=F32) * SCALE
            slot = lax.broadcasted_iota(jnp.int32, (QROWS, CHUNK), 1) + start
            part = jnp.where(slot < length[s], part, -jnp.inf)
            scores[s, :, pl.ds(start, CHUNK)] = part
            for j in range(CHUNK // HEAD_DIM):
                largest = jnp.maximum(largest, part[:, j * HEAD_DIM : (j + 1) * HEAD_DIM])
            return largest

        largest = lax.fori_loop(0, SLOTS // CHUNK, body, jnp.full((QROWS, HEAD_DIM), -jnp.inf, F32))
        return jnp.max(largest, axis=1, keepdims=True)

    def weigh(s, top):
        loads[7 + s].wait()

        def body(i, carry):
            total, acc = carry
            start = pl.multiple_of(i * CHUNK, CHUNK)
            p = jnp.exp(scores[s, :, pl.ds(start, CHUNK)] - top)
            for j in range(CHUNK // HEAD_DIM):
                total = total + p[:, j * HEAD_DIM : (j + 1) * HEAD_DIM]
            high = p.astype(BF16)
            both = jnp.concatenate([high, (p - high.astype(F32)).astype(BF16)], axis=0)
            out = jnp.dot(both, vbuf[s, pl.ds(start, CHUNK), :], preferred_element_type=F32)
            return total, acc + (out[:QROWS] + out[QROWS:])

        zero = jnp.zeros((QROWS, HEAD_DIM), F32)
        total, acc = lax.fori_loop(0, SLOTS // CHUNK, body, (zero, zero))
        return jnp.sum(total, axis=1, keepdims=True), acc

    top = [None, None]
    total = [None, None]
    acc = [None, None]
    top[0] = score(0)
    top[1] = score(1)

    pltpu.make_async_copy(hrecv.at[pl.ds(0, REPS - 1)], hrecv.at[pl.ds(0, REPS - 1)], small_recv.at[0]).wait()
    for r in range(REPS):
        for t in range(STEPS):
            hall[pl.ds(r * TOKENS + t * SESSIONS, SESSIONS), :] = hrecv[r, t].astype(F32)
    product = jnp.dot(hall[...].astype(BF16), pooled[rep], preferred_element_type=F32)
    for r in range(REPS):
        psend[r] = product[r * TOKENS : (r + 1) * TOKENS, :].astype(BF16)

    @pl.loop(1, REPS)
    def _(k):
        peer = lax.rem(rep + k, REPS)
        small(psend.at[peer], precv.at[rep], 1, (peer, tp)).start()

    precv[rep] = psend[rep]

    events(0, 1)
    events(2)
    total[0], acc[0] = weigh(0, top[0])
    total[1], acc[1] = weigh(1, top[1])
    events(3, 4)


    row = lax.broadcasted_iota(jnp.int32, (TOKENS, HEAD_DIM), 0)
    lane = lax.broadcasted_iota(jnp.int32, (TOKENS, HEAD_DIM), 1)
    position = jnp.where(row % 2 == 0, length[0], length[1]) + row // 2
    angle = position.astype(F32) * frequencies((TOKENS, HEAD_DIM))
    cosine = jnp.cos(angle)
    sine = jnp.where(lane < HEAD_DIM // 2, -jnp.sin(angle), jnp.sin(angle))
    lhs[...] = jnp.zeros(lhs.shape, F32)

    @pl.when(rep == COLLECTOR)
    def _():
        pl.semaphore_wait(barrier, TPS - 1)

        @pl.loop(0, REPS)
        def _(k):
            @pl.when(k != COLLECTOR)
            def _():
                pl.semaphore_signal(ready, inc=1, device_id=(k, tp), device_id_type=MESH)

    pltpu.make_async_copy(precv.at[pl.ds(0, REPS - 1)], precv.at[pl.ds(0, REPS - 1)], small_recv.at[1]).wait()
    projected = precv[0].astype(F32)
    for r in range(1, REPS):
        projected = projected + precv[r].astype(F32)
    raw = projected[:, :HEAD_DIM]
    swapped = jnp.concatenate([raw[:, HEAD_DIM // 2 :], raw[:, : HEAD_DIM // 2]], axis=1)
    new_keys = (raw * cosine + swapped * sine).astype(BF16)
    new_values = projected[:, HEAD_DIM:].astype(BF16)
    for t in range(STEPS):
        appended[t, :, pl.ds(0, HEAD_DIM)] = new_keys[t * SESSIONS : (t + 1) * SESSIONS, :]
        appended[t, :, pl.ds(HEAD_DIM, HEAD_DIM)] = new_values[t * SESSIONS : (t + 1) * SESSIONS, :]
    new_keys = new_keys.astype(F32)
    new_values = new_values.astype(F32)
    second = lax.broadcasted_iota(jnp.int32, (QROWS, 1), 0) >= GROUP
    for s in range(SESSIONS):
        q = qrows[s]
        fresh = [
            jnp.sum(q * new_keys[u * SESSIONS + s : u * SESSIONS + s + 1, :], axis=1, keepdims=True) * SCALE
            for u in range(STEPS)]
        fresh[1] = jnp.where(second, fresh[1], -jnp.inf)
        peak = jnp.maximum(top[s], jnp.maximum(fresh[0], fresh[1]))
        keep = jnp.exp(top[s] - peak)
        fresh = [jnp.exp(x - peak) for x in fresh]
        whole = total[s] * keep + fresh[0] + fresh[1]
        out = acc[s] * (keep / whole)
        for u in range(STEPS):
            out = out + (fresh[u] / whole).astype(BF16).astype(F32) * new_values[u * SESSIONS + s : u * SESSIONS + s + 1, :]
        heads[s] = out
    for s in range(SESSIONS):
        for t in range(STEPS):
            for q in range(GROUP):
                lhs[pl.ds(t * SESSIONS + s, 1), pl.ds(q * HEAD_DIM, HEAD_DIM)] = heads[s, pl.ds(t * GROUP + q, 1), :]
    events(5, 6)
    left = lhs[...].astype(BF16)
    loads[9].wait()

    @pl.when(rep != COLLECTOR)
    def _():
        pl.semaphore_wait(ready, 1)

    for part in range(PARTS):
        @pl.loop(0, PART // OUT_COLS)
        def _(i):
            start = pl.multiple_of(i * OUT_COLS, OUT_COLS)
            result = jnp.dot(left, wbuf[:, pl.ds(part * PART + start, OUT_COLS)], preferred_element_type=F32)
            osend[part, :, pl.ds(start, OUT_COLS)] = result[:TOKENS].astype(BF16)

        @pl.loop(1, TPS)
        def _(k):
            small(osend.at[part], orecv.at[part, tp], 2, (rep, lax.rem(tp + k, TPS))).start()

    events(17)
    events(7, 8)
    events(11, 12)
    events(13, 14)
    events(9, 10)
    events(15, 16)

    def drain(ref, sem):
        pltpu.make_async_copy(ref, ref, sem).wait()

    arrived(there[2], A0_END, 18)
    arrived(far_other, A0_END, 19)
    arrived(there[2], A1_END, 20)
    arrived(far_other, A1_END, 21)
    others = orecv.at[:, pl.ds(0, TPS - 1)]
    drain(others, small_recv.at[2])
    for part in range(PARTS):
        orecv[part, tp] = osend[part]
        for i in range(PART // OUT_COLS):
            columns = pl.ds(i * OUT_COLS, OUT_COLS)
            summed = orecv[part, 0, :, columns].astype(F32)
            for r in range(1, TPS):
                summed = summed + orecv[part, r, :, columns].astype(F32)
            summed = summed.astype(BF16)
            for t in range(STEPS):
                attended[t, :, pl.ds(part * PART + i * OUT_COLS, OUT_COLS)] = summed[t * SESSIONS : (t + 1) * SESSIONS, :]
    drain(pooled.at[pl.ds(0, REPS // 2), pl.ds(0, ROWS - 16)], sib_recv)
    drain(pooled.at[pl.ds(0, REPS - 1)], bulk_send)
    drain(hsend.at[pl.ds(0, REPS - 1)], small_send.at[0])
    drain(psend.at[pl.ds(0, REPS - 1)], small_send.at[1])
    drain(others, small_send.at[2])


def write_kernel(owners, pooled, attended, appended, installed, attended_out, appended_out, sem):
    copies = [
        pltpu.make_async_copy(pooled.at[owners[s]], installed.at[s], sem.at[s]) for s in range(REPS)]
    copies.append(pltpu.make_async_copy(attended, attended_out, sem.at[REPS]))
    copies.append(pltpu.make_async_copy(appended, appended_out, sem.at[REPS + 1]))
    for copy in copies:
        copy.start()
    for copy in copies:
        copy.wait()


def shards(hidden, queries, sectioned, owners, keys, values, lengths, weight):
    operands = [
        pltpu.with_memory_space_constraint(x, pltpu.HBM)
        for x in (hidden, queries, sectioned, owners, keys, values, lengths, weight)]
    hbm = pl.BlockSpec(memory_space=pltpu.HBM)
    vmem = pl.BlockSpec(memory_space=pltpu.VMEM)
    pooled, attended, appended = pl.pallas_call(
        main_kernel,
        out_shape=(
            pltpu.VMEM((REPS, ROWS, COLS), BF16),
            pltpu.VMEM((STEPS, SESSIONS, PARTS * PART), BF16),
            pltpu.VMEM((STEPS, SESSIONS, COLS), BF16),
        ),
        in_specs=[hbm] * 8,
        out_specs=(vmem, vmem, vmem),
        scratch_shapes=[
            pltpu.VMEM((SESSIONS, SLOTS, HEAD_DIM), BF16),
            pltpu.VMEM((SESSIONS, SLOTS, HEAD_DIM), BF16),
            pltpu.VMEM((GROUP * HEAD_DIM, PARTS * PART), BF16),
            pltpu.VMEM((STEPS, SESSIONS, REPS * ROWS), BF16),
            pltpu.VMEM((STEPS, SESSIONS, GROUP * HEAD_DIM), BF16),
            pltpu.SMEM((REPS,), jnp.int32),
            pltpu.SMEM((SESSIONS,), jnp.int32),
            pltpu.VMEM((REPS, STEPS, SESSIONS, ROWS), BF16),
            pltpu.VMEM((REPS, STEPS, SESSIONS, ROWS), BF16),
            pltpu.VMEM((REPS, STEPS, SESSIONS, ROWS), BF16),
            pltpu.VMEM((REPS * TOKENS, ROWS), F32),
            pltpu.VMEM((REPS, TOKENS, COLS), BF16),
            pltpu.VMEM((REPS, TOKENS, COLS), BF16),
            pltpu.VMEM((SESSIONS, QROWS, HEAD_DIM), F32),
            pltpu.VMEM((SESSIONS, QROWS, SLOTS), F32),
            pltpu.VMEM((SESSIONS, QROWS, HEAD_DIM), F32),
            pltpu.VMEM((8, GROUP * HEAD_DIM), F32),
            pltpu.VMEM((PARTS, TOKENS, PART), BF16),
            pltpu.VMEM((PARTS, TPS, TOKENS, PART), BF16),
            pltpu.SemaphoreType.DMA((10,)),
            pltpu.SemaphoreType.DMA,
            pltpu.SemaphoreType.DMA((22,)),
            pltpu.SemaphoreType.DMA,
            pltpu.SemaphoreType.DMA((3,)),
            pltpu.SemaphoreType.DMA((3,)),
            pltpu.SemaphoreType.REGULAR,
        ],
        compiler_params=pltpu.CompilerParams(
            collective_id=0, has_side_effects=True, vmem_limit_bytes=32 << 20),
        name="gather_and_attend",
    )(*operands)
    installed, attended, appended = pl.pallas_call(
        write_kernel,
        out_shape=(
            jax.ShapeDtypeStruct((REPS, ROWS, COLS), BF16),
            jax.ShapeDtypeStruct(attended.shape, BF16),
            jax.ShapeDtypeStruct(appended.shape, BF16),
        ),
        grid_spec=pltpu.PrefetchScalarGridSpec(
            num_scalar_prefetch=1,
            grid=(),
            in_specs=[vmem, vmem, vmem],
            out_specs=(hbm, hbm, hbm),
            scratch_shapes=[pltpu.SemaphoreType.DMA((REPS + 2,))],
        ),
        compiler_params=pltpu.CompilerParams(vmem_limit_bytes=4 << 20),
        name="write_in_order",
    )(owners, pooled, attended, appended)
    return installed.reshape(REPS * ROWS, COLS), appended, attended


def solution(mesh):
    in_specs = (
        P(None, "rep", None),
        P(None, "rep", "tp"),
        P("rep", "tp"),
        P(),
        P("rep", None, "tp"),
        P("rep", None, "tp"),
        P("rep"),
        P("tp", None),
    )
    out_specs = (P(None, "tp"), P(None, "rep", "tp"), P(None, "rep", None))
    return jax.shard_map(shards, mesh=mesh, in_specs=in_specs, out_specs=out_specs, check_vma=False)
```

```python
import functools
import math

import jax
import jax.numpy as jnp
from jax import lax
from jax.experimental import pallas as pl
from jax.experimental.pallas import tpu as pltpu
from jax.sharding import PartitionSpec as P

HEAD_DIM = 128
ROPE_BASE = 500000.0
SCALE = HEAD_DIM**-0.5
MESH = pl.DeviceIdType.MESH
F32 = jnp.float32
BF16 = jnp.bfloat16

REPS = 16
HERALD = 2
COLLECTOR = 3
TPS = 8
ROWS = 512
COLS = 256
STEPS = 2
SESSIONS = 2
TOKENS = STEPS * SESSIONS
GROUP = 8
QROWS = STEPS * GROUP
SLOTS = 8192
CHUNK = 2048
OUT_COLS = 512
PARTS = 4
PART = 1024

A0 = (0, 160)
A1 = (160, 176)
A = (0, 336)
B0 = (336, 80)
B1 = (416, 96)
B = (336, 176)
A0_MOST, A0_END = (0, 96), (96, 64)
A1_MOST, A1_END = (160, 112), (272, 64)
WHOLE = (0, 512)


def frequencies(shape):
    lane = lax.broadcasted_iota(jnp.int32, shape, 1) % (HEAD_DIM // 2)
    result = jnp.ones(shape, F32)
    for bit in range(6):
        factor = math.exp(-math.log(ROPE_BASE) * (1 << bit) / (HEAD_DIM // 2))
        result = result * jnp.where((lane // (1 << bit)) % 2 == 1, factor, 1.0).astype(F32)
    return result


def main_kernel(
    hidden, queries, sectioned, owners, keys, values, lengths, weight,
    pooled, attended, appended,
    kbuf, vbuf, wbuf, hbuf, qbuf, own_s, len_s, hsplit, hsend, hrecv, hall, psend, precv,
    qrows, scores, heads, lhs, osend, orecv,
    load_sem, bulk_send, bulk_recv, sib_recv, small_send, small_recv, ready,
):
    rep = lax.axis_index("rep")
    tp = lax.axis_index("tp")
    y, z, c = rep // 8, (rep // 2) % 4, rep % 2

    def chip(yy, zz, cc):
        return yy * 8 + lax.rem(zz + 4, 4) * 2 + cc

    zp = (chip(y, z + 1, c), tp)
    zm = (chip(y, z - 1, c), tp)
    yn = (chip(1 - y, z, c), tp)
    sib = (chip(y, z, 1 - c), tp)
    zp_other = (chip(y, z + 1, 1 - c), tp)
    zm_other = (chip(y, z - 1, 1 - c), tp)
    far_other = chip(1 - y, z + 2, 1 - c)

    barrier = pltpu.get_barrier_semaphore()

    @pl.loop(0, REPS)
    def _(k):
        @pl.when((k != rep) & (k != COLLECTOR))
        def _():
            pl.semaphore_signal(barrier, inc=1, device_id=(k, tp), device_id_type=MESH)

    loads = [
        pltpu.make_async_copy(owners, own_s, load_sem.at[0]),
        pltpu.make_async_copy(hidden, hbuf, load_sem.at[1]),
        pltpu.make_async_copy(sectioned, pooled.at[rep], load_sem.at[2]),
        pltpu.make_async_copy(lengths, len_s, load_sem.at[3]),
        pltpu.make_async_copy(queries, qbuf, load_sem.at[4]),
        pltpu.make_async_copy(keys.at[0], kbuf.at[0], load_sem.at[5]),
        pltpu.make_async_copy(keys.at[1], kbuf.at[1], load_sem.at[6]),
        pltpu.make_async_copy(values.at[0], vbuf.at[0], load_sem.at[7]),
        pltpu.make_async_copy(values.at[1], vbuf.at[1], load_sem.at[8]),
        pltpu.make_async_copy(weight, wbuf, load_sem.at[9]),
    ]
    for load in loads[:5]:
        load.start()

    loads[1].wait()
    for r in range(REPS):
        for t in range(STEPS):
            hsplit[r, t] = hbuf[t, :, pl.ds(r * ROWS, ROWS)]
    loads[0].wait()
    owner = [own_s[s] for s in range(REPS)]
    for r in range(REPS):
        found = jnp.int32(0)
        for s in range(1, REPS):
            found = jnp.where(owner[s] == r, s, found)
        hsend[r] = hsplit[found]

    loads[2].wait()
    for load in loads[5:]:
        load.start()

    @pl.when(rep != COLLECTOR)
    def _():
        pl.semaphore_wait(barrier, REPS - 1)

    @pl.when(rep == HERALD)
    def _():
        pl.semaphore_signal(ready, inc=1, device_id=(COLLECTOR, tp), device_id_type=MESH)

    @pl.when(rep == COLLECTOR)
    def _():
        pl.semaphore_wait(ready, 1)

    def small(src, dst, which, device):
        return pltpu.make_async_remote_copy(
            src_ref=src, dst_ref=dst, send_sem=small_send.at[which], recv_sem=small_recv.at[which],
            device_id=device, device_id_type=MESH)

    @pl.loop(1, REPS)
    def _(k):
        peer = lax.rem(rep + k, REPS)
        small(hsend.at[peer], hrecv.at[rep], 0, (peer, tp)).start()

    hrecv[rep] = hsend[rep]

    def piece(block, part):
        return pooled.at[block, pl.ds(*part), :]

    def send(block, part, device, slot):
        ref = piece(block, part)
        pltpu.make_async_remote_copy(
            src_ref=ref, dst_ref=ref, send_sem=bulk_send, recv_sem=bulk_recv.at[slot],
            device_id=device, device_id_type=MESH).start()

    def to_sibling(block, part):
        ref = piece(block, part)
        pltpu.make_async_remote_copy(
            src_ref=ref, dst_ref=ref, send_sem=bulk_send, recv_sem=sib_recv,
            device_id=sib, device_id_type=MESH).start()

    def arrived(block, part, slot):
        ref = piece(block, part)
        pltpu.make_async_copy(ref, ref, bulk_recv.at[slot]).wait()

    here = {
        0: chip(y, z, c), 1: chip(y, z + 1, c), -1: chip(y, z - 1, c), 2: chip(y, z + 2, c)}
    there = {
        0: chip(1 - y, z, c), 1: chip(1 - y, z + 1, c), -1: chip(1 - y, z - 1, c), 2: chip(1 - y, z + 2, c)}

    route = [
        (here[-1], B, [(zp, B0, 5), (yn, B, 7)]),
        (here[1], B, [(zm, B1, 6), (yn, B, 8)]),
        (there[0], A, [(zp, A, 11), (zm, A, 12)]),
        (here[-1], A, [(zp, A0, 13)]),
        (here[1], A, [(zm, A1, 14)]),
        (here[2], B0, [(yn, B0, 9)]),
        (here[2], B1, [(yn, B1, 10)]),
        (there[-1], B, []),
        (there[1], B, []),
        (there[2], B0, []),
        (there[2], B1, []),
        (there[-1], A, [(zp, A0_MOST, 15), (zp, A0_END, 18), (zp_other, A0_END, 19)]),
        (there[1], A, [(zm, A1_MOST, 16), (zm, A1_END, 20), (zm_other, A1_END, 21)]),
        (here[2], A0, []),
        (here[2], A1, []),
        (there[2], A0_MOST, []),
        (there[2], A1_MOST, []),
        (there[0], B, []),
    ]

    def events(*slots):
        for n in slots:
            block, part, onward = route[n]
            arrived(block, part, n)
            for device, onward_part, slot in onward:
                send(block, onward_part, device, slot)
        done = [(route[n][0], route[n][1]) for n in slots]
        if len(done) == 2 and done[0][0] is done[1][0] and sum(done[0][1]) == done[1][1][0]:
            to_sibling(done[0][0], (done[0][1][0], done[0][1][1] + done[1][1][1]))
        else:
            for block, part in done:
                to_sibling(block, part)

    send(here[0], B, zp, 0)
    send(here[0], B, zm, 1)
    send(here[0], A, yn, 2)
    send(here[0], A, zp, 3)
    send(here[0], A, zm, 4)
    send(here[0], B, yn, 17)
    to_sibling(here[0], WHOLE)

    @pl.when(rep == HERALD)
    def _():
        @pl.loop(1, TPS)
        def _(k):
            pl.semaphore_signal(barrier, inc=1, device_id=(COLLECTOR, lax.rem(tp + k, TPS)), device_id_type=MESH)

    loads[3].wait()
    length = [len_s[s] for s in range(SESSIONS)]
    loads[4].wait()
    for s in range(SESSIONS):
        for t in range(STEPS):
            for q in range(GROUP):
                qrows[s, pl.ds(t * GROUP + q, 1), :] = qbuf[t, pl.ds(s, 1), pl.ds(q * HEAD_DIM, HEAD_DIM)].astype(F32)

    def score(s):
        loads[5 + s].wait()
        q = qrows[s].astype(BF16)

        def body(i, largest):
            start = pl.multiple_of(i * CHUNK, CHUNK)
            part = lax.dot_general(
                q, kbuf[s, pl.ds(start, CHUNK), :], (((1,), (1,)), ((), ())), preferred_element_type=F32) * SCALE
            slot = lax.broadcasted_iota(jnp.int32, (QROWS, CHUNK), 1) + start
            part = jnp.where(slot < length[s], part, -jnp.inf)
            scores[s, :, pl.ds(start, CHUNK)] = part
            for j in range(CHUNK // HEAD_DIM):
                largest = jnp.maximum(largest, part[:, j * HEAD_DIM : (j + 1) * HEAD_DIM])
            return largest

        largest = lax.fori_loop(0, SLOTS // CHUNK, body, jnp.full((QROWS, HEAD_DIM), -jnp.inf, F32))
        return jnp.max(largest, axis=1, keepdims=True)

    def weigh(s, top):
        loads[7 + s].wait()

        def body(i, carry):
            total, acc = carry
            start = pl.multiple_of(i * CHUNK, CHUNK)
            p = jnp.exp(scores[s, :, pl.ds(start, CHUNK)] - top)
            for j in range(CHUNK // HEAD_DIM):
                total = total + p[:, j * HEAD_DIM : (j + 1) * HEAD_DIM]
            acc = acc + jnp.dot(p.astype(BF16), vbuf[s, pl.ds(start, CHUNK), :], preferred_element_type=F32)
            return total, acc

        zero = jnp.zeros((QROWS, HEAD_DIM), F32)
        total, acc = lax.fori_loop(0, SLOTS // CHUNK, body, (zero, zero))
        return jnp.sum(total, axis=1, keepdims=True), acc

    top = [None, None]
    total = [None, None]
    acc = [None, None]
    top[0] = score(0)
    top[1] = score(1)

    pltpu.make_async_copy(hrecv.at[pl.ds(0, REPS - 1)], hrecv.at[pl.ds(0, REPS - 1)], small_recv.at[0]).wait()
    for r in range(REPS):
        for t in range(STEPS):
            hall[pl.ds(r * TOKENS + t * SESSIONS, SESSIONS), :] = hrecv[r, t].astype(F32)
    product = jnp.dot(hall[...].astype(BF16), pooled[rep], preferred_element_type=F32)
    for r in range(REPS):
        psend[r] = product[r * TOKENS : (r + 1) * TOKENS, :].astype(BF16)

    @pl.loop(1, REPS)
    def _(k):
        peer = lax.rem(rep + k, REPS)
        small(psend.at[peer], precv.at[rep], 1, (peer, tp)).start()

    precv[rep] = psend[rep]

    events(0, 1)
    events(2)
    total[0], acc[0] = weigh(0, top[0])
    total[1], acc[1] = weigh(1, top[1])
    events(3, 4)


    row = lax.broadcasted_iota(jnp.int32, (TOKENS, HEAD_DIM), 0)
    lane = lax.broadcasted_iota(jnp.int32, (TOKENS, HEAD_DIM), 1)
    position = jnp.where(row % 2 == 0, length[0], length[1]) + row // 2
    angle = position.astype(F32) * frequencies((TOKENS, HEAD_DIM))
    cosine = jnp.cos(angle)
    sine = jnp.where(lane < HEAD_DIM // 2, -jnp.sin(angle), jnp.sin(angle))
    lhs[...] = jnp.zeros(lhs.shape, F32)

    @pl.when(rep == COLLECTOR)
    def _():
        pl.semaphore_wait(barrier, TPS - 1)

        @pl.loop(0, REPS)
        def _(k):
            @pl.when(k != COLLECTOR)
            def _():
                pl.semaphore_signal(ready, inc=1, device_id=(k, tp), device_id_type=MESH)

    pltpu.make_async_copy(precv.at[pl.ds(0, REPS - 1)], precv.at[pl.ds(0, REPS - 1)], small_recv.at[1]).wait()
    projected = precv[0].astype(F32)
    for r in range(1, REPS):
        projected = projected + precv[r].astype(F32)
    raw = projected[:, :HEAD_DIM]
    swapped = jnp.concatenate([raw[:, HEAD_DIM // 2 :], raw[:, : HEAD_DIM // 2]], axis=1)
    new_keys = (raw * cosine + swapped * sine).astype(BF16)
    new_values = projected[:, HEAD_DIM:].astype(BF16)
    for t in range(STEPS):
        appended[t, :, pl.ds(0, HEAD_DIM)] = new_keys[t * SESSIONS : (t + 1) * SESSIONS, :]
        appended[t, :, pl.ds(HEAD_DIM, HEAD_DIM)] = new_values[t * SESSIONS : (t + 1) * SESSIONS, :]
    new_keys = new_keys.astype(F32)
    new_values = new_values.astype(F32)
    second = lax.broadcasted_iota(jnp.int32, (QROWS, 1), 0) >= GROUP
    for s in range(SESSIONS):
        q = qrows[s]
        fresh = [
            jnp.sum(q * new_keys[u * SESSIONS + s : u * SESSIONS + s + 1, :], axis=1, keepdims=True) * SCALE
            for u in range(STEPS)]
        fresh[1] = jnp.where(second, fresh[1], -jnp.inf)
        peak = jnp.maximum(top[s], jnp.maximum(fresh[0], fresh[1]))
        keep = jnp.exp(top[s] - peak)
        fresh = [jnp.exp(x - peak) for x in fresh]
        whole = total[s] * keep + fresh[0] + fresh[1]
        out = acc[s] * (keep / whole)
        for u in range(STEPS):
            out = out + (fresh[u] / whole).astype(BF16).astype(F32) * new_values[u * SESSIONS + s : u * SESSIONS + s + 1, :]
        heads[s] = out
    for s in range(SESSIONS):
        for t in range(STEPS):
            for q in range(GROUP):
                lhs[pl.ds(t * SESSIONS + s, 1), pl.ds(q * HEAD_DIM, HEAD_DIM)] = heads[s, pl.ds(t * GROUP + q, 1), :]
    events(5, 6)
    left = lhs[...].astype(BF16)
    loads[9].wait()

    @pl.when(rep != COLLECTOR)
    def _():
        pl.semaphore_wait(ready, 1)

    for part in range(PARTS):
        @pl.loop(0, PART // OUT_COLS)
        def _(i):
            start = pl.multiple_of(i * OUT_COLS, OUT_COLS)
            result = jnp.dot(left, wbuf[:, pl.ds(part * PART + start, OUT_COLS)], preferred_element_type=F32)
            osend[part, :, pl.ds(start, OUT_COLS)] = result[:TOKENS].astype(BF16)

        @pl.loop(1, TPS)
        def _(k):
            small(osend.at[part], orecv.at[part, tp], 2, (rep, lax.rem(tp + k, TPS))).start()

    events(17)
    events(7, 8)
    events(11, 12)
    events(13, 14)
    events(9, 10)
    events(15, 16)

    def drain(ref, sem):
        pltpu.make_async_copy(ref, ref, sem).wait()

    arrived(there[2], A0_END, 18)
    arrived(far_other, A0_END, 19)
    arrived(there[2], A1_END, 20)
    arrived(far_other, A1_END, 21)
    others = orecv.at[:, pl.ds(0, TPS - 1)]
    drain(others, small_recv.at[2])
    for part in range(PARTS):
        orecv[part, tp] = osend[part]
        for i in range(PART // OUT_COLS):
            columns = pl.ds(i * OUT_COLS, OUT_COLS)
            summed = orecv[part, 0, :, columns].astype(F32)
            for r in range(1, TPS):
                summed = summed + orecv[part, r, :, columns].astype(F32)
            summed = summed.astype(BF16)
            for t in range(STEPS):
                attended[t, :, pl.ds(part * PART + i * OUT_COLS, OUT_COLS)] = summed[t * SESSIONS : (t + 1) * SESSIONS, :]
    drain(pooled.at[pl.ds(0, REPS // 2), pl.ds(0, ROWS - 16)], sib_recv)
    drain(pooled.at[pl.ds(0, REPS - 1)], bulk_send)
    drain(hsend.at[pl.ds(0, REPS - 1)], small_send.at[0])
    drain(psend.at[pl.ds(0, REPS - 1)], small_send.at[1])
    drain(others, small_send.at[2])


def write_kernel(owners, pooled, attended, appended, installed, attended_out, appended_out, sem):
    copies = [
        pltpu.make_async_copy(pooled.at[owners[s]], installed.at[s], sem.at[s]) for s in range(REPS)]
    copies.append(pltpu.make_async_copy(attended, attended_out, sem.at[REPS]))
    copies.append(pltpu.make_async_copy(appended, appended_out, sem.at[REPS + 1]))
    for copy in copies:
        copy.start()
    for copy in copies:
        copy.wait()


def shards(hidden, queries, sectioned, owners, keys, values, lengths, weight):
    operands = [
        pltpu.with_memory_space_constraint(x, pltpu.HBM)
        for x in (hidden, queries, sectioned, owners, keys, values, lengths, weight)]
    hbm = pl.BlockSpec(memory_space=pltpu.HBM)
    vmem = pl.BlockSpec(memory_space=pltpu.VMEM)
    pooled, attended, appended = pl.pallas_call(
        main_kernel,
        out_shape=(
            pltpu.VMEM((REPS, ROWS, COLS), BF16),
            pltpu.VMEM((STEPS, SESSIONS, PARTS * PART), BF16),
            pltpu.VMEM((STEPS, SESSIONS, COLS), BF16),
        ),
        in_specs=[hbm] * 8,
        out_specs=(vmem, vmem, vmem),
        scratch_shapes=[
            pltpu.VMEM((SESSIONS, SLOTS, HEAD_DIM), BF16),
            pltpu.VMEM((SESSIONS, SLOTS, HEAD_DIM), BF16),
            pltpu.VMEM((GROUP * HEAD_DIM, PARTS * PART), BF16),
            pltpu.VMEM((STEPS, SESSIONS, REPS * ROWS), BF16),
            pltpu.VMEM((STEPS, SESSIONS, GROUP * HEAD_DIM), BF16),
            pltpu.SMEM((REPS,), jnp.int32),
            pltpu.SMEM((SESSIONS,), jnp.int32),
            pltpu.VMEM((REPS, STEPS, SESSIONS, ROWS), BF16),
            pltpu.VMEM((REPS, STEPS, SESSIONS, ROWS), BF16),
            pltpu.VMEM((REPS, STEPS, SESSIONS, ROWS), BF16),
            pltpu.VMEM((REPS * TOKENS, ROWS), F32),
            pltpu.VMEM((REPS, TOKENS, COLS), BF16),
            pltpu.VMEM((REPS, TOKENS, COLS), BF16),
            pltpu.VMEM((SESSIONS, QROWS, HEAD_DIM), F32),
            pltpu.VMEM((SESSIONS, QROWS, SLOTS), F32),
            pltpu.VMEM((SESSIONS, QROWS, HEAD_DIM), F32),
            pltpu.VMEM((8, GROUP * HEAD_DIM), F32),
            pltpu.VMEM((PARTS, TOKENS, PART), BF16),
            pltpu.VMEM((PARTS, TPS, TOKENS, PART), BF16),
            pltpu.SemaphoreType.DMA((10,)),
            pltpu.SemaphoreType.DMA,
            pltpu.SemaphoreType.DMA((22,)),
            pltpu.SemaphoreType.DMA,
            pltpu.SemaphoreType.DMA((3,)),
            pltpu.SemaphoreType.DMA((3,)),
            pltpu.SemaphoreType.REGULAR,
        ],
        compiler_params=pltpu.CompilerParams(
            collective_id=0, has_side_effects=True, vmem_limit_bytes=32 << 20),
        name="gather_and_attend",
    )(*operands)
    installed, attended, appended = pl.pallas_call(
        write_kernel,
        out_shape=(
            jax.ShapeDtypeStruct((REPS, ROWS, COLS), BF16),
            jax.ShapeDtypeStruct(attended.shape, BF16),
            jax.ShapeDtypeStruct(appended.shape, BF16),
        ),
        grid_spec=pltpu.PrefetchScalarGridSpec(
            num_scalar_prefetch=1,
            grid=(),
            in_specs=[vmem, vmem, vmem],
            out_specs=(hbm, hbm, hbm),
            scratch_shapes=[pltpu.SemaphoreType.DMA((REPS + 2,))],
        ),
        compiler_params=pltpu.CompilerParams(vmem_limit_bytes=4 << 20),
        name="write_in_order",
    )(owners, pooled, attended, appended)
    return installed.reshape(REPS * ROWS, COLS), appended, attended


def solution(mesh):
    in_specs = (
        P(None, "rep", None),
        P(None, "rep", "tp"),
        P("rep", "tp"),
        P(),
        P("rep", None, "tp"),
        P("rep", None, "tp"),
        P("rep"),
        P("tp", None),
    )
    out_specs = (P(None, "tp"), P(None, "rep", "tp"), P(None, "rep", None))
    return jax.shard_map(shards, mesh=mesh, in_specs=in_specs, out_specs=out_specs, check_vma=False)
```
